32 devices in a mesh: groups: 2 (over x), seq: 16 (over z, y, core).
Axes of the slice: x: 2, y: 2, z: 4, core: 2. Of those that a mesh axis runs over, the one named last changes fastest.
Arguments:
- queries: bfloat16 [4096, 5120], P(('groups', 'seq')), parts along dimension 0, may hold values from -12 to 12
- keys: bfloat16 [4096, 5120], P(('groups', 'seq')), parts along dimension 0, may hold values from -12 to 12
- values: bfloat16 [4096, 5120], P(('groups', 'seq')), parts along dimension 0, may hold values from -6 to 6
- q_gain: float32 [5120], replicated, may hold values from 0.1 to 1.9
- k_gain: float32 [5120], replicated, may hold values from 0.1 to 1.9
- key_tiles: int32 [40, 16, 16], replicated, may hold values from 0 to 15, as said below
- key_count: int32 [40, 16], replicated, may hold values from 1 to 16
Outputs:
- attended: bfloat16 [4096, 5120], P(('groups', 'seq')), parts along dimension 0
The draws below stay inside these ranges and needn't reach their ends.
There are 2 independent parts, one for each index of `groups`. The reference program is written for one: setup_inputs(seed, part) draws one part's arguments, and reference() takes and returns one part's arrays. A program takes and returns all parts, laid end to end along the dimension named above; an argument that names none is the same for every part. Nothing has to cross between parts.
Inputs may be any that keep to these rules, and one draw needn't show every extreme that they name: key_tiles[h, t] holds 16 distinct tiles and its first entry is t itself.
All inputs are finite; a program needn't handle non-finite values.
Results may differ from the reference program's by a relative error of at most 0.012.
The reference program's roundings to bfloat16 on the way count: a program that leaves them out, or rounds other values in their place, can miss the bound.
Values may be sent and summed in bfloat16 or wider, within the bound.
No kernel may reach another device: no remote copies, remote signals or barrier semaphores. Data moves between devices by JAX's collectives and lax.ppermute only.
A program may use at most 128 MiB of HBM per device.

```python
import math
import jax
import jax.numpy as jnp
from jax import lax

D = 5120
HEADS = 40
HEAD_DIM = 128
TILE = 128
KEEP = 16
TILES = 16
TOKENS = 2048


def pair_rows(key):
    key_parts = jax.random.split(jax.random.fold_in(key, 7), 3)
    col_scale = jnp.exp(jax.random.uniform(key_parts[0], (D,), jnp.float32, math.log(0.3), math.log(3.0)))
    query_rows = jnp.clip(jax.random.normal(key_parts[1], (TOKENS, D), jnp.float32), -4.0, 4.0) * col_scale
    key_rows = jnp.clip(jax.random.normal(key_parts[2], (TOKENS, D), jnp.float32), -4.0, 4.0) * col_scale
    return (query_rows, key_rows)


def draw_queries(key, part):
    return pair_rows(key)[0].astype(jnp.bfloat16)


def draw_keys(key, part):
    return pair_rows(key)[1].astype(jnp.bfloat16)


def draw_key_tiles(key, part):
    random_draws = jax.random.randint(jax.random.fold_in(key, 11), (HEADS, TILES, TILES), 0, 1 << 20)
    column = jnp.arange(TILES)
    ranking = random_draws * TILES + column[None, None, :]
    ranking = jnp.where(column[None, None, :] == column[None, :, None], 1 << 30, ranking)
    return lax.top_k(ranking, KEEP)[1].astype(jnp.int32)


def draw_key_count(key, part):
    key_parts = jax.random.split(jax.random.fold_in(key, 13), 3)
    lowest = jax.random.randint(key_parts[0], (HEADS, 1), 1, KEEP + 1)
    random_draws = jax.random.randint(key_parts[1], (HEADS, TILES), 0, 1 << 20)
    counts = random_draws % (KEEP - lowest + 1) + lowest
    places = jax.random.randint(key_parts[2], (2,), 0, HEADS * TILES)
    top_place = places[0]
    low_place = (places[0] + 1 + places[1] % (HEADS * TILES - 1)) % (HEADS * TILES)
    flattened = counts.reshape(-1)
    position = jnp.arange(HEADS * TILES)
    flattened = jnp.where(position == top_place, KEEP, jnp.where(position == low_place, 1, flattened))
    return flattened.reshape(HEADS, TILES).astype(jnp.int32)


def levels(stream_key, extent, shards, smallest, top_value):
    factor_of, own = 1.0, jax.random.fold_in(stream_key, 6)
    for axis_at, blocks in shards:
        draws = jnp.exp(jax.random.uniform(jax.random.fold_in(own, axis_at), (blocks,), jnp.float32, smallest / len(shards), top_value / len(shards)))
        factor_of = factor_of * jnp.repeat(draws, extent[axis_at] // blocks).reshape([-1 if axis == axis_at else 1 for axis in range(len(extent))])
    return factor_of


def gaussian(stream_key, dims, width, reach, cuts=(), kind=jnp.bfloat16):
    entries = jax.random.normal(stream_key, dims, jnp.float32) * width
    if len(cuts) > 0:
        entries = levels(stream_key, dims, cuts, -0.22, 0.18) * entries
    return jnp.clip(entries, min=-reach, max=reach).astype(kind)


def setup_inputs(seed: int = 0, part: int = 0) -> dict:
    arg_keys = jax.random.split(jax.random.key(seed), 8)
    part_splits = jax.random.split(jax.random.fold_in(arg_keys[7], part), 8)
    return {
        "queries": draw_queries(jax.random.fold_in(jax.random.fold_in(arg_keys[7], part), 71), part),
        "keys": draw_keys(jax.random.fold_in(jax.random.fold_in(arg_keys[7], part), 71), part),
        "values": gaussian(part_splits[2], (TOKENS, D), 1.0, 6.0, ((0, 16),)),
        "q_gain": jnp.clip(1.0 + 0.18 * jax.random.normal(arg_keys[3], (D,), jnp.float32), 0.1, 1.9),
        "k_gain": jnp.clip(1.0 + 0.18 * jax.random.normal(arg_keys[4], (D,), jnp.float32), 0.1, 1.9),
        "key_tiles": draw_key_tiles(jax.random.fold_in(arg_keys[7], 71), part),
        "key_count": draw_key_count(jax.random.fold_in(arg_keys[7], 71), part),
    }


def normed(rows, gain):
    values32 = rows.astype(jnp.float32)
    factor = lax.rsqrt(lax.optimization_barrier(jnp.mean(values32 * values32, axis=-1, keepdims=True)) + 1e-06)
    return (values32 * factor * gain).astype(jnp.bfloat16)

def attend(query_rows, key_block, value_block, counts):
    units = query_rows.shape[0]
    tile_rows = query_rows.shape[1]
    key_flat = key_block.reshape(units, -1, key_block.shape[-1]).astype(jnp.float32)
    value_flat = value_block.reshape(units, -1, value_block.shape[-1]).astype(jnp.float32)
    scores = jnp.einsum('uqd,ukd->uqk', query_rows.astype(jnp.float32), key_flat) / math.sqrt(query_rows.shape[-1])
    list_place = jnp.arange(key_flat.shape[1]) // tile_rows
    valid = (list_place[None, :] < counts[:, None])[:, None, :]
    masked = jnp.where(valid, scores, -jnp.inf)
    peak = lax.optimization_barrier(jnp.max(masked, axis=-1, keepdims=True))
    weights = jnp.where(valid, jnp.exp(masked - peak), jnp.float32(0.0))
    total = lax.optimization_barrier(jnp.sum(weights, axis=-1, keepdims=True))
    probs = weights.astype(jnp.bfloat16)
    mixed = jnp.einsum('uqk,ukd->uqd', probs.astype(jnp.float32), value_flat) / total
    return mixed.astype(jnp.bfloat16)

def reference(queries, keys, values, q_gain, k_gain, key_tiles, key_count):
    q_split = normed(queries, q_gain).reshape(TILES, TILE, HEADS, HEAD_DIM).transpose(2, 0, 1, 3)
    k_split = normed(keys, k_gain).reshape(TILES, TILE, HEADS, HEAD_DIM).transpose(2, 0, 1, 3)
    v_split = values.reshape(TILES, TILE, HEADS, HEAD_DIM).transpose(2, 0, 1, 3)

    def per_head(head_items):
        q_head, k_head, v_head, key_lists, counts = head_items
        return attend(q_head, k_head[key_lists], v_head[key_lists], counts)
    result = lax.map(per_head, (q_split, k_split, v_split, key_tiles, key_count))
    return result.transpose(1, 2, 0, 3).reshape(TOKENS, D)
```

```python
import functools
import math

import jax
import jax.numpy as jnp
from jax import lax
from jax.experimental import pallas as pl
from jax.experimental.pallas import tpu as pltpu
from jax.sharding import PartitionSpec as P

HEADS = 40
HEAD_DIM = 128
TILE = 128


group_size = 4


def normed(rows, gain):
    values32 = rows.astype(jnp.float32)
    factor = lax.rsqrt(jnp.mean(values32 * values32, axis=-1, keepdims=True) + 1e-06)
    return (values32 * factor * gain).astype(jnp.bfloat16)


def padded(entries, length):
    return jnp.pad(entries, (0, length - entries.shape[0]), mode="edge")


def attend_units(received, slot_index, tile_index, head_index, key_tiles, key_count):

    def one_group(unit_items):
        slot_part, tile_part, head_part = unit_items
        query_rows = received[tile_part, slot_part, 0]
        key_lists = key_tiles[head_part, tile_part]
        counts = key_count[head_part, tile_part]
        key_block = received[key_lists, slot_part[:, None], 1]
        value_block = received[key_lists, slot_part[:, None], 2]
        units = query_rows.shape[0]
        tile_rows = query_rows.shape[1]
        key_flat = key_block.reshape(units, -1, key_block.shape[-1])
        value_flat = value_block.reshape(units, -1, value_block.shape[-1])
        scores = jnp.einsum(
            "uqd,ukd->uqk", query_rows, key_flat, preferred_element_type=jnp.float32
        ) / math.sqrt(query_rows.shape[-1])
        list_place = jnp.arange(key_flat.shape[1]) // tile_rows
        valid = (list_place[None, :] < counts[:, None])[:, None, :]
        masked = jnp.where(valid, scores, -jnp.inf)
        peak = jnp.max(masked, axis=-1, keepdims=True)
        weights = jnp.where(valid, jnp.exp(masked - peak), jnp.float32(0.0))
        total = jnp.sum(weights, axis=-1, keepdims=True)
        probs = weights.astype(jnp.bfloat16)
        mixed = (
            jnp.einsum("uqk,ukd->uqd", probs, value_flat, preferred_element_type=jnp.float32)
            / total
        )
        return mixed.astype(jnp.bfloat16)

    grouped = (
        slot_index.reshape(-1, group_size),
        tile_index.reshape(-1, group_size),
        head_index.reshape(-1, group_size),
    )
    result = lax.map(one_group, grouped)
    return result.reshape(-1, result.shape[2], result.shape[3])


def local_general(queries, keys, values, q_gain, k_gain, key_tiles, key_count):
    devices = lax.axis_size("seq")
    my_index = lax.axis_index("seq")
    q_normed = normed(queries, q_gain)
    k_normed = normed(keys, k_gain)
    stacked = (
        jnp.stack([q_normed, k_normed, values])
        .reshape(3, TILE, HEADS, HEAD_DIM)
        .transpose(2, 0, 1, 3)
    )
    targets = jnp.arange(devices)
    per_device = (HEADS + devices - 1) // devices
    total_slots = devices * per_device
    fewest_slots = total_slots // HEADS
    most_units = (devices + fewest_slots - 1) // fewest_slots

    def slot_layout(slot_number):
        head_of = slot_number * HEADS // total_slots
        head_start = (head_of * total_slots + HEADS - 1) // HEADS
        head_end = ((head_of + 1) * total_slots + HEADS - 1) // HEADS
        sharers = head_end - head_start
        within = slot_number - head_start
        return (head_of, within * devices // sharers, (within + 1) * devices // sharers)

    all_slots = jnp.arange(total_slots).reshape(devices, per_device)
    send_heads = slot_layout(all_slots)[0]
    received = lax.all_to_all(stacked[send_heads], "seq", split_axis=0, concat_axis=0, tiled=True)
    own_heads, lower_tile, upper_tile = slot_layout(my_index * per_device + jnp.arange(per_device))
    offsets = jnp.arange(most_units)
    tile_grid = jnp.minimum(lower_tile[:, None] + offsets[None, :], devices - 1)
    slot_grid = jnp.broadcast_to(jnp.arange(per_device)[:, None], tile_grid.shape)
    head_grid = jnp.broadcast_to(own_heads[:, None], tile_grid.shape)
    unit_total = per_device * most_units
    length = (unit_total + group_size - 1) // group_size * group_size
    finished = attend_units(
        received,
        padded(slot_grid.reshape(-1), length),
        padded(tile_grid.reshape(-1), length),
        padded(head_grid.reshape(-1), length),
        key_tiles,
        key_count,
    )[:unit_total]
    finished = finished.reshape(per_device, most_units, TILE, HEAD_DIM)
    position = targets[:, None] - lower_tile[None, :]
    inside = (position >= 0) & (targets[:, None] < upper_tile[None, :])
    gathered = finished[jnp.arange(per_device)[None, :], jnp.clip(position, 0, most_units - 1)]
    outgoing = jnp.where(inside[:, :, None, None], gathered, jnp.zeros_like(gathered))
    returned = lax.all_to_all(outgoing, "seq", split_axis=0, concat_axis=0, tiled=True)
    head_list = jnp.arange(HEADS)
    head_start = (head_list * total_slots + HEADS - 1) // HEADS
    sharers = ((head_list + 1) * total_slots + HEADS - 1) // HEADS - head_start
    owner_slot = head_start + ((my_index + 1) * sharers - 1) // devices
    pieces = returned[owner_slot // per_device, owner_slot % per_device]
    return pieces.transpose(1, 0, 2).reshape(TILE, HEADS * HEAD_DIM)


HALF = TILE // 2
VMEM_BYTES = 48 * 1024 * 1024


def pair_layout(devices):
    per_pair = 2 * HEADS // devices
    full = per_pair // 2
    places = []
    for head in range(HEADS):
        pair, within = divmod(head, per_pair)
        if within < full:
            places.append([(2 * pair, within)])
        elif within >= per_pair - full:
            places.append([(2 * pair + 1, within - (per_pair - full))])
        else:
            places.append([(2 * pair, full), (2 * pair + 1, full)])
    return places, full


def put_head(parts, places, head, block):
    holders = places[head]
    for which, (device, slot) in enumerate(holders):
        if slot not in parts:
            continue
        ref, unit = parts[slot]
        if len(holders) == 2:
            ref[device, unit] = block[which * HALF : (which + 1) * HALF]
        else:
            ref[device, unit] = block[:HALF]
            ref[device, unit + 1] = block[HALF:]


def head_columns(head):
    return slice(head * HEAD_DIM, (head + 1) * HEAD_DIM)


def normed_blocks(rows_ref, gain_ref):
    squares = jnp.zeros((TILE, HEAD_DIM), jnp.float32)
    for head in range(HEADS):
        block = rows_ref[:, head_columns(head)].astype(jnp.float32)
        squares = squares + block * block
    mean = jnp.sum(squares, axis=-1, keepdims=True) / (HEADS * HEAD_DIM)
    factor = lax.rsqrt(mean + 1e-06)
    for head in range(HEADS):
        block = rows_ref[:, head_columns(head)].astype(jnp.float32)
        yield head, (block * factor * gain_ref[:, head_columns(head)]).astype(jnp.bfloat16)


def values_kernel(places, full, values_ref, out_ref):
    parts = {slot: (out_ref, 2 * slot) for slot in range(full + 1)}
    for head in range(HEADS):
        put_head(parts, places, head, values_ref[:, head_columns(head)])


def norm_kernel(
    places, full, early, queries_ref, keys_ref, q_gain_ref, k_gain_ref, first_ref, second_ref
):
    query_parts = {
        slot: (first_ref, 2 * slot) if slot < early else (second_ref, 2 * (slot - early))
        for slot in range(full + 1)
    }
    key_parts = {slot: (first_ref, 2 * (early + slot)) for slot in range(full + 1)}
    for head, block in normed_blocks(keys_ref, k_gain_ref):
        put_head(key_parts, places, head, block)
    for head, block in normed_blocks(queries_ref, q_gain_ref):
        put_head(query_parts, places, head, block)


def attend_rows(queries, keys, values, masks):
    rows = queries[0].shape[0]
    tiles = keys.shape[0] // TILE
    stacked = jnp.concatenate(queries, axis=0)
    scores = lax.dot_general(
        stacked, keys, (((1,), (1,)), ((), ())), preferred_element_type=jnp.float32
    )
    scale = jnp.float32(math.log2(math.e) / math.sqrt(HEAD_DIM))
    probs, totals = [], []
    for i, mask in enumerate(masks):
        parts = []
        for tile in range(tiles):
            offset = jnp.where((mask >> tile) & 1 == 1, jnp.float32(0.0), jnp.float32(-1e30))
            part = scores[i * rows : (i + 1) * rows, tile * TILE : (tile + 1) * TILE]
            parts.append(part + offset)
        peak = jnp.max(functools.reduce(jnp.maximum, parts), axis=-1, keepdims=True)
        weights = [jnp.exp2((part - peak) * scale) for part in parts]
        totals.append(jnp.sum(functools.reduce(jnp.add, weights), axis=-1, keepdims=True))
        probs.append(jnp.concatenate([w.astype(jnp.bfloat16) for w in weights], axis=1))
    mixed = jnp.dot(jnp.concatenate(probs, axis=0), values, preferred_element_type=jnp.float32)
    return [
        (mixed[i * rows : (i + 1) * rows] / totals[i]).astype(jnp.bfloat16)
        for i in range(len(masks))
    ]


def attend_head(mask_ref, mask_row, query_at, keys_at, values_at, store, tiles, together):
    def step(index, carry):
        first = index * together
        out = attend_rows(
            [query_at(first + i) for i in range(together)],
            keys_at(),
            values_at(),
            [mask_ref[mask_row, first + i] for i in range(together)],
        )
        for i in range(together):
            store(first + i, out[i])
        return carry

    lax.fori_loop(0, tiles // together, step, 0)


def whole_head(ref, unit):
    return ref[:, unit : unit + 2].reshape(-1, HEAD_DIM)


def whole_heads(mask_ref, heads, query_ref, first_ref, value_ref, out_ref, query_slot, early):
    tiles = query_ref.shape[0]
    for row, slot in heads:
        unit = 2 * (slot - query_slot)

        def store(tile, block, unit=unit):
            out_ref[tile, unit] = block[:HALF]
            out_ref[tile, unit + 1] = block[HALF:]

        attend_head(
            mask_ref,
            row,
            lambda tile, unit=unit: query_ref[tile, unit : unit + 2].reshape(TILE, HEAD_DIM),
            lambda slot=slot: whole_head(first_ref, 2 * (early + slot)),
            lambda slot=slot: whole_head(value_ref, 2 * slot),
            store,
            tiles,
            2,
        )


def early_kernel(early, mask_ref, first_ref, value_ref, out_ref):
    heads = [(slot, slot) for slot in range(early)]
    whole_heads(mask_ref, heads, first_ref, first_ref, value_ref, out_ref, 0, early)


def late_kernel(
    early,
    full,
    mask_ref,
    second_ref,
    first_ref,
    value_ref,
    other_key_ref,
    other_value_ref,
    out_ref,
    key_scratch,
    value_scratch,
):
    heads = [(slot, slot) for slot in range(early, full)]
    whole_heads(mask_ref, heads, second_ref, first_ref, value_ref, out_ref, early, early)
    key_scratch[:, 0] = first_ref[:, 2 * (early + full)]
    key_scratch[:, 1] = other_key_ref[...]
    value_scratch[:, 0] = value_ref[:, 2 * full]
    value_scratch[:, 1] = other_value_ref[...]
    unit = 2 * (full - early)

    def store(tile, block):
        out_ref[tile, unit] = block

    attend_head(
        mask_ref,
        full,
        lambda tile: second_ref[tile, unit],
        lambda: whole_head(key_scratch, 0),
        lambda: whole_head(value_scratch, 0),
        store,
        second_ref.shape[0],
        4,
    )


def collect_kernel(places, early, early_ref, late_ref, out_ref):
    for head in range(HEADS):
        for which, (device, slot) in enumerate(places[head]):
            ref, unit = (early_ref, 2 * slot) if slot < early else (late_ref, 2 * (slot - early))
            columns = head_columns(head)
            if len(places[head]) == 2:
                out_ref[which * HALF : (which + 1) * HALF, columns] = ref[device, unit]
            else:
                out_ref[:HALF, columns] = ref[device, unit]
                out_ref[HALF:, columns] = ref[device, unit + 1]


def on_chip(kernel, name, out_shapes, *operands, smem=0, scratch=()):
    in_vmem = pl.BlockSpec(memory_space=pltpu.VMEM)
    in_smem = pl.BlockSpec(memory_space=pltpu.SMEM)
    outs = [jax.ShapeDtypeStruct(shape, jnp.bfloat16) for shape in out_shapes]
    return pl.pallas_call(
        kernel,
        name=name,
        out_shape=outs,
        in_specs=[in_smem] * smem + [in_vmem] * (len(operands) - smem),
        out_specs=[in_vmem] * len(outs),
        scratch_shapes=list(scratch),
        compiler_params=pltpu.CompilerParams(vmem_limit_bytes=VMEM_BYTES),
    )(*operands)


def exchange(blocks):
    return lax.all_to_all(blocks, "seq", split_axis=0, concat_axis=0, tiled=True)


def after(value, *others):
    return lax.optimization_barrier((value, *others))[0]


def local_paired(queries, keys, values, q_gain, k_gain, key_tiles, key_count):
    devices = lax.axis_size("seq")
    my_index = lax.axis_index("seq")
    places, full = pair_layout(devices)
    early = full // 2
    units = 2 * full + 1
    swap = [(i, i ^ 1) for i in range(devices)]

    def buffer(count):
        return (devices, count, HALF, HEAD_DIM)

    (value_send,) = on_chip(
        functools.partial(values_kernel, places, full), "lay_out_values", [buffer(units)], values
    )
    value_here = exchange(value_send)
    first_send, second_send = on_chip(
        functools.partial(norm_kernel, places, full, early),
        "norm",
        [buffer(2 * early + units), buffer(units - 2 * early)],
        queries,
        keys,
        q_gain.reshape(1, -1),
        k_gain.reshape(1, -1),
    )
    allowed = jnp.arange(key_tiles.shape[-1]) < key_count[:, :, None]
    masks = jnp.sum(jnp.where(allowed, jnp.left_shift(1, key_tiles), 0), axis=-1)
    pair, core = my_index // 2, my_index % 2
    slots = jnp.arange(full + 1)
    within = jnp.where(slots < full, slots + core * (full + 1), full)
    masks = masks[pair * (2 * full + 1) + within]

    first_here = exchange(after(first_send, value_here))
    other_values = lax.ppermute(value_here[:, 2 * full], "seq", swap)
    second_here = exchange(after(second_send, first_here))
    other_keys = lax.ppermute(first_here[:, 2 * (early + full)], "seq", swap)
    (early_out,) = on_chip(
        functools.partial(early_kernel, early),
        "attend_early",
        [buffer(2 * early)],
        masks,
        first_here,
        value_here,
        smem=1,
    )
    early_back = exchange(after(early_out, second_here))
    shared = pltpu.VMEM((devices, 2, HALF, HEAD_DIM), jnp.bfloat16)
    (late_out,) = on_chip(
        functools.partial(late_kernel, early, full),
        "attend_late",
        [buffer(units - 2 * early)],
        masks,
        second_here,
        first_here,
        value_here,
        other_keys,
        other_values,
        smem=1,
        scratch=[shared, shared],
    )
    late_back = exchange(after(late_out, early_back))
    (attended,) = on_chip(
        functools.partial(collect_kernel, places, early),
        "collect",
        [queries.shape],
        early_back,
        late_back,
    )
    return attended


def paired_fits(mesh, key_tiles_shape):
    devices = mesh.shape["seq"]
    per_pair, rest = divmod(2 * HEADS, devices)
    return (
        devices % 2 == 0
        and rest == 0
        and per_pair % 2 == 1
        and per_pair >= 5
        and devices % 4 == 0
        and key_tiles_shape[1] == devices
        and devices <= 31
    )


def solution(mesh):
    in_specs = (
        P(("groups", "seq"), None),
        P(("groups", "seq"), None),
        P(("groups", "seq"), None),
        P(),
        P(),
        P(),
        P(),
    )
    out_specs = P(("groups", "seq"), None)

    def run(*operands):
        paired = paired_fits(mesh, operands[5].shape)
        body = local_paired if paired else local_general
        return jax.shard_map(
            body, mesh=mesh, in_specs=in_specs, out_specs=out_specs, check_vma=False
        )(*operands)

    return run
```

```python
import functools
import math

import jax
import jax.numpy as jnp
from jax import lax
from jax.experimental import pallas as pl
from jax.experimental.pallas import tpu as pltpu
from jax.sharding import PartitionSpec as P

HEADS = 40
HEAD_DIM = 128
TILE = 128


group_size = 4


def normed(rows, gain):
    values32 = rows.astype(jnp.float32)
    factor = lax.rsqrt(jnp.mean(values32 * values32, axis=-1, keepdims=True) + 1e-06)
    return (values32 * factor * gain).astype(jnp.bfloat16)


def padded(entries, length):
    return jnp.pad(entries, (0, length - entries.shape[0]), mode="edge")


def attend_units(received, slot_index, tile_index, head_index, key_tiles, key_count):

    def one_group(unit_items):
        slot_part, tile_part, head_part = unit_items
        query_rows = received[tile_part, slot_part, 0]
        key_lists = key_tiles[head_part, tile_part]
        counts = key_count[head_part, tile_part]
        key_block = received[key_lists, slot_part[:, None], 1]
        value_block = received[key_lists, slot_part[:, None], 2]
        units = query_rows.shape[0]
        tile_rows = query_rows.shape[1]
        key_flat = key_block.reshape(units, -1, key_block.shape[-1])
        value_flat = value_block.reshape(units, -1, value_block.shape[-1])
        scores = jnp.einsum(
            "uqd,ukd->uqk", query_rows, key_flat, preferred_element_type=jnp.float32
        ) / math.sqrt(query_rows.shape[-1])
        list_place = jnp.arange(key_flat.shape[1]) // tile_rows
        valid = (list_place[None, :] < counts[:, None])[:, None, :]
        masked = jnp.where(valid, scores, -jnp.inf)
        peak = jnp.max(masked, axis=-1, keepdims=True)
        weights = jnp.where(valid, jnp.exp(masked - peak), jnp.float32(0.0))
        total = jnp.sum(weights, axis=-1, keepdims=True)
        probs = weights.astype(jnp.bfloat16)
        mixed = (
            jnp.einsum("uqk,ukd->uqd", probs, value_flat, preferred_element_type=jnp.float32)
            / total
        )
        return mixed.astype(jnp.bfloat16)

    grouped = (
        slot_index.reshape(-1, group_size),
        tile_index.reshape(-1, group_size),
        head_index.reshape(-1, group_size),
    )
    result = lax.map(one_group, grouped)
    return result.reshape(-1, result.shape[2], result.shape[3])


def local_general(queries, keys, values, q_gain, k_gain, key_tiles, key_count):
    devices = lax.axis_size("seq")
    my_index = lax.axis_index("seq")
    q_normed = normed(queries, q_gain)
    k_normed = normed(keys, k_gain)
    stacked = (
        jnp.stack([q_normed, k_normed, values])
        .reshape(3, TILE, HEADS, HEAD_DIM)
        .transpose(2, 0, 1, 3)
    )
    targets = jnp.arange(devices)
    per_device = (HEADS + devices - 1) // devices
    total_slots = devices * per_device
    fewest_slots = total_slots // HEADS
    most_units = (devices + fewest_slots - 1) // fewest_slots

    def slot_layout(slot_number):
        head_of = slot_number * HEADS // total_slots
        head_start = (head_of * total_slots + HEADS - 1) // HEADS
        head_end = ((head_of + 1) * total_slots + HEADS - 1) // HEADS
        sharers = head_end - head_start
        within = slot_number - head_start
        return (head_of, within * devices // sharers, (within + 1) * devices // sharers)

    all_slots = jnp.arange(total_slots).reshape(devices, per_device)
    send_heads = slot_layout(all_slots)[0]
    received = lax.all_to_all(stacked[send_heads], "seq", split_axis=0, concat_axis=0, tiled=True)
    own_heads, lower_tile, upper_tile = slot_layout(my_index * per_device + jnp.arange(per_device))
    offsets = jnp.arange(most_units)
    tile_grid = jnp.minimum(lower_tile[:, None] + offsets[None, :], devices - 1)
    slot_grid = jnp.broadcast_to(jnp.arange(per_device)[:, None], tile_grid.shape)
    head_grid = jnp.broadcast_to(own_heads[:, None], tile_grid.shape)
    unit_total = per_device * most_units
    length = (unit_total + group_size - 1) // group_size * group_size
    finished = attend_units(
        received,
        padded(slot_grid.reshape(-1), length),
        padded(tile_grid.reshape(-1), length),
        padded(head_grid.reshape(-1), length),
        key_tiles,
        key_count,
    )[:unit_total]
    finished = finished.reshape(per_device, most_units, TILE, HEAD_DIM)
    position = targets[:, None] - lower_tile[None, :]
    inside = (position >= 0) & (targets[:, None] < upper_tile[None, :])
    gathered = finished[jnp.arange(per_device)[None, :], jnp.clip(position, 0, most_units - 1)]
    outgoing = jnp.where(inside[:, :, None, None], gathered, jnp.zeros_like(gathered))
    returned = lax.all_to_all(outgoing, "seq", split_axis=0, concat_axis=0, tiled=True)
    head_list = jnp.arange(HEADS)
    head_start = (head_list * total_slots + HEADS - 1) // HEADS
    sharers = ((head_list + 1) * total_slots + HEADS - 1) // HEADS - head_start
    owner_slot = head_start + ((my_index + 1) * sharers - 1) // devices
    pieces = returned[owner_slot // per_device, owner_slot % per_device]
    return pieces.transpose(1, 0, 2).reshape(TILE, HEADS * HEAD_DIM)


HALF = TILE // 2
VMEM_BYTES = 48 * 1024 * 1024


def pair_layout(devices):
    per_pair = 2 * HEADS // devices
    full = per_pair // 2
    places = []
    for head in range(HEADS):
        pair, within = divmod(head, per_pair)
        if within < full:
            places.append([(2 * pair, within)])
        elif within >= per_pair - full:
            places.append([(2 * pair + 1, within - (per_pair - full))])
        else:
            places.append([(2 * pair, full), (2 * pair + 1, full)])
    return places, full


def slot_rows(slots, full, pieces):
    rows, at = {}, 0
    for slot in slots:
        rows[slot] = at
        at += pieces * (HALF if slot == full else TILE)
    return rows, at


def head_columns(head):
    return slice(head * HEAD_DIM, (head + 1) * HEAD_DIM)


def prepare_kernel(
    places,
    full,
    slots,
    queries_ref,
    keys_ref,
    values_ref,
    q_gain_ref,
    k_gain_ref,
    out_ref,
    query_rows,
    key_rows,
    staged,
    in_sems,
    value_sems,
    out_sems,
):
    base, _ = slot_rows(slots, full, 3)
    halves = [slice(0, HALF), slice(HALF, TILE)]
    loads = {}
    for i, (source, rows) in enumerate([(keys_ref, key_rows), (queries_ref, query_rows)]):
        for half in range(2):
            loads[i, half] = pltpu.make_async_copy(
                source.at[halves[half]], rows.at[halves[half]], in_sems.at[2 * i + half]
            )
            loads[i, half].start()
    copies = []
    for head in range(HEADS):
        for which, (device, slot) in enumerate(places[head]):
            if slot not in base:
                continue
            if slot == full:
                source = values_ref.at[halves[which], head_columns(head)]
                target = out_ref.at[device, pl.ds(base[slot] + 2 * HALF, HALF)]
            else:
                source = values_ref.at[:, head_columns(head)]
                target = out_ref.at[device, pl.ds(base[slot] + 2 * TILE, TILE)]
            copies.append(pltpu.make_async_copy(source, target, value_sems.at[len(copies)]))
            copies[-1].start()
    sent = 0
    for i, (rows, gain_ref, piece) in enumerate(
        [(key_rows, k_gain_ref, 1), (query_rows, q_gain_ref, 0)]
    ):
        for half in range(2):
            loads[i, half].wait()
            squares = jnp.zeros((HALF, HEAD_DIM), jnp.float32)
            for head in range(HEADS):
                block = rows[halves[half], head_columns(head)].astype(jnp.float32)
                squares = squares + block * block
            mean = jnp.sum(squares, axis=-1, keepdims=True) / (HEADS * HEAD_DIM)
            factor = lax.rsqrt(mean + 1e-06)
            for head in range(HEADS):
                for which, (device, slot) in enumerate(places[head]):
                    if slot not in base or (slot == full and which != half):
                        continue
                    block = rows[halves[half], head_columns(head)].astype(jnp.float32)
                    gain = gain_ref[head_columns(head)][None, :]
                    done = (block * factor * gain).astype(jnp.bfloat16)
                    if slot == full:
                        first = base[slot] + piece * HALF
                    else:
                        first = base[slot] + piece * TILE + half * HALF
                    staged[device, first : first + HALF] = done
            for slot in slots:
                if slot == full and half == 0:
                    continue
                if slot == full:
                    here = pl.ds(base[slot] + piece * HALF, HALF)
                else:
                    here = pl.ds(base[slot] + piece * TILE + half * HALF, HALF)
                copies.append(
                    pltpu.make_async_copy(
                        staged.at[:, here], out_ref.at[:, here], out_sems.at[sent]
                    )
                )
                copies[-1].start()
                sent += 1
    for copy in copies:
        copy.wait()


def prepare(places, full, slots, devices, queries, keys, values, q_gain, k_gain):
    rows = slot_rows(slots, full, 3)[1]
    value_copies = sum(slot in slots for holders in places for _, slot in holders)
    out_copies = sum(2 if slot == full else 4 for slot in slots)
    anywhere = pl.BlockSpec(memory_space=pl.ANY)
    in_vmem = pl.BlockSpec(memory_space=pltpu.VMEM)
    return pl.pallas_call(
        functools.partial(prepare_kernel, places, full, slots),
        name="prepare",
        out_shape=jax.ShapeDtypeStruct((devices, rows, HEAD_DIM), jnp.bfloat16),
        in_specs=[anywhere] * 3 + [in_vmem] * 2,
        out_specs=anywhere,
        scratch_shapes=[
            pltpu.VMEM(queries.shape, jnp.bfloat16),
            pltpu.VMEM(keys.shape, jnp.bfloat16),
            pltpu.VMEM((devices, rows, HEAD_DIM), jnp.bfloat16),
            pltpu.SemaphoreType.DMA((4,)),
            pltpu.SemaphoreType.DMA((value_copies,)),
            pltpu.SemaphoreType.DMA((out_copies,)),
        ],
        compiler_params=pltpu.CompilerParams(vmem_limit_bytes=VMEM_BYTES),
    )(queries, keys, values, q_gain, k_gain)


def attend_rows(queries, keys, values, masks):
    rows = queries[0].shape[0]
    tiles = keys.shape[0] // TILE
    stacked = jnp.concatenate(queries, axis=0)
    scores = lax.dot_general(
        stacked, keys, (((1,), (1,)), ((), ())), preferred_element_type=jnp.float32
    )
    scale = jnp.float32(math.log2(math.e) / math.sqrt(HEAD_DIM))
    probs, totals = [], []
    for i, mask in enumerate(masks):
        parts = []
        for tile in range(tiles):
            offset = jnp.where((mask >> tile) & 1 == 1, jnp.float32(0.0), jnp.float32(-1e30))
            part = scores[i * rows : (i + 1) * rows, tile * TILE : (tile + 1) * TILE]
            parts.append(part + offset)
        peak = jnp.max(functools.reduce(jnp.maximum, parts), axis=-1, keepdims=True)
        weights = [jnp.exp2((part - peak) * scale) for part in parts]
        totals.append(jnp.sum(functools.reduce(jnp.add, weights), axis=-1, keepdims=True))
        probs.append(jnp.concatenate([w.astype(jnp.bfloat16) for w in weights], axis=1))
    mixed = jnp.dot(jnp.concatenate(probs, axis=0), values, preferred_element_type=jnp.float32)
    return [
        (mixed[i * rows : (i + 1) * rows] / totals[i]).astype(jnp.bfloat16)
        for i in range(len(masks))
    ]


def attend_head(mask_ref, slot, here_ref, first, keys_at, values_at, out_ref, out_first, rows):
    tiles = here_ref.shape[0]
    together = 2 * TILE // rows

    def step(index, carry):
        at = index * together
        out = attend_rows(
            [here_ref[at + i, first : first + rows] for i in range(together)],
            keys_at(),
            values_at(),
            [mask_ref[slot, at + i] for i in range(together)],
        )
        for i in range(together):
            out_ref[at + i, out_first : out_first + rows] = out[i]
        return carry

    lax.fori_loop(0, tiles // together, step, 0)


def attend_kernel(full, slots, mask_ref, here_ref, *refs):
    base, _ = slot_rows(slots, full, 3)
    out_base, _ = slot_rows(slots, full, 1)
    if full in slots:
        other_ref, out_ref, shared_keys, shared_values = refs
    else:
        (out_ref,) = refs
    for slot in slots:
        first = base[slot]
        if slot == full:
            shared_keys[:, :HALF] = here_ref[:, first + HALF : first + 2 * HALF]
            shared_keys[:, HALF:] = other_ref[:, :HALF]
            shared_values[:, :HALF] = here_ref[:, first + 2 * HALF : first + 3 * HALF]
            shared_values[:, HALF:] = other_ref[:, HALF:]
            attend_head(
                mask_ref,
                slot,
                here_ref,
                first,
                lambda: shared_keys[...].reshape(-1, HEAD_DIM),
                lambda: shared_values[...].reshape(-1, HEAD_DIM),
                out_ref,
                out_base[slot],
                HALF,
            )
        else:
            keys, values = (slice(first + i * TILE, first + (i + 1) * TILE) for i in (1, 2))
            attend_head(
                mask_ref,
                slot,
                here_ref,
                first,
                lambda keys=keys: here_ref[:, keys].reshape(-1, HEAD_DIM),
                lambda values=values: here_ref[:, values].reshape(-1, HEAD_DIM),
                out_ref,
                out_base[slot],
                TILE,
            )


def attend_slots(full, slots, masks, here, *other):
    in_vmem = pl.BlockSpec(memory_space=pltpu.VMEM)
    in_smem = pl.BlockSpec(memory_space=pltpu.SMEM)
    devices = here.shape[0]
    rows = slot_rows(slots, full, 1)[1]
    shared = pltpu.VMEM((devices, TILE, HEAD_DIM), jnp.bfloat16)
    return pl.pallas_call(
        functools.partial(attend_kernel, full, slots),
        name="attend",
        out_shape=jax.ShapeDtypeStruct((devices, rows, HEAD_DIM), jnp.bfloat16),
        in_specs=[in_smem] + [in_vmem] * (1 + len(other)),
        out_specs=in_vmem,
        scratch_shapes=[shared, shared] if other else [],
        compiler_params=pltpu.CompilerParams(vmem_limit_bytes=VMEM_BYTES),
    )(masks, here, *other)


def collect_kernel(places, full, slots, here_ref, *refs):
    out_ref, sems = refs[-2:]
    base, _ = slot_rows(slots, full, 1)
    copies = []
    for head in range(HEADS):
        for which, (device, slot) in enumerate(places[head]):
            if slot not in base:
                continue
            rows = pl.ds(which * HALF, HALF) if slot == full else pl.ds(0, TILE)
            copies.append(
                pltpu.make_async_copy(
                    here_ref.at[device, pl.ds(base[slot], HALF if slot == full else TILE)],
                    out_ref.at[rows, head_columns(head)],
                    sems.at[len(copies)],
                )
            )
            copies[-1].start()
    for copy in copies:
        copy.wait()


def collect(places, full, slots, shape, here, *so_far):
    anywhere = pl.BlockSpec(memory_space=pl.ANY)
    count = sum(slot in slots for holders in places for _, slot in holders)
    return pl.pallas_call(
        functools.partial(collect_kernel, places, full, slots),
        name="collect",
        out_shape=jax.ShapeDtypeStruct(shape, jnp.bfloat16),
        in_specs=[anywhere] * (1 + len(so_far)),
        out_specs=anywhere,
        scratch_shapes=[pltpu.SemaphoreType.DMA((count,))],
        input_output_aliases={1: 0} if so_far else {},
        compiler_params=pltpu.CompilerParams(vmem_limit_bytes=VMEM_BYTES),
    )(here, *so_far)


def exchange(blocks):
    return lax.all_to_all(blocks, "seq", split_axis=0, concat_axis=0, tiled=True)


def after(value, *others):
    return lax.optimization_barrier((value, *others))[0]


def local_paired(queries, keys, values, q_gain, k_gain, key_tiles, key_count):
    devices = lax.axis_size("seq")
    my_index = lax.axis_index("seq")
    places, full = pair_layout(devices)
    late = tuple(range(full - full // 2, full))
    early = tuple(range(full - full // 2)) + (full,)
    swap = [(i, i ^ 1) for i in range(devices)]

    operands = (queries, keys, values, q_gain, k_gain)
    early_here = exchange(prepare(places, full, early, devices, *operands))
    late_send = prepare(places, full, late, devices, *operands)

    allowed = jnp.arange(key_tiles.shape[-1]) < key_count[:, :, None]
    masks = jnp.sum(jnp.where(allowed, jnp.left_shift(1, key_tiles), 0), axis=-1)
    pair, core = my_index // 2, my_index % 2
    slots = jnp.arange(full + 1)
    within = jnp.where(slots < full, slots + core * (full + 1), full)
    masks = masks[pair * (2 * full + 1) + within]

    late_here = exchange(after(late_send, early_here))
    shared_first = slot_rows(early, full, 3)[0][full]
    own = early_here[:, shared_first + HALF : shared_first + 3 * HALF]
    other = lax.ppermute(own, "seq", swap)
    early_out = attend_slots(full, early, masks, early_here, other)
    early_back = exchange(after(early_out, late_here))
    late_out = attend_slots(full, late, masks, late_here)
    late_back = exchange(after(late_out, early_back))
    so_far = collect(places, full, early, queries.shape, early_back)
    return collect(places, full, late, queries.shape, late_back, so_far)


def paired_fits(mesh, key_tiles_shape):
    devices = mesh.shape["seq"]
    per_pair, rest = divmod(2 * HEADS, devices)
    return (
        rest == 0
        and per_pair % 2 == 1
        and per_pair >= 5
        and devices % 4 == 0
        and key_tiles_shape[1] == devices
        and devices <= 31
    )


def solution(mesh):
    in_specs = (
        P(("groups", "seq"), None),
        P(("groups", "seq"), None),
        P(("groups", "seq"), None),
        P(),
        P(),
        P(),
        P(),
    )
    out_specs = P(("groups", "seq"), None)

    def run(*operands):
        paired = paired_fits(mesh, operands[5].shape)
        body = local_paired if paired else local_general
        return jax.shard_map(
            body, mesh=mesh, in_specs=in_specs, out_specs=out_specs, check_vma=False
        )(*operands)

    return run
```

```python
import functools
import math

import jax
import jax.numpy as jnp
from jax import lax
from jax.experimental import pallas as pl
from jax.experimental.pallas import tpu as pltpu
from jax.sharding import PartitionSpec as P

HEADS = 40
HEAD_DIM = 128
TILE = 128


group_size = 4


def normed(rows, gain):
    values32 = rows.astype(jnp.float32)
    factor = lax.rsqrt(jnp.mean(values32 * values32, axis=-1, keepdims=True) + 1e-06)
    return (values32 * factor * gain).astype(jnp.bfloat16)


def padded(entries, length):
    return jnp.pad(entries, (0, length - entries.shape[0]), mode="edge")


def attend_units(received, slot_index, tile_index, head_index, key_tiles, key_count):

    def one_group(unit_items):
        slot_part, tile_part, head_part = unit_items
        query_rows = received[tile_part, slot_part, 0]
        key_lists = key_tiles[head_part, tile_part]
        counts = key_count[head_part, tile_part]
        key_block = received[key_lists, slot_part[:, None], 1]
        value_block = received[key_lists, slot_part[:, None], 2]
        units = query_rows.shape[0]
        tile_rows = query_rows.shape[1]
        key_flat = key_block.reshape(units, -1, key_block.shape[-1])
        value_flat = value_block.reshape(units, -1, value_block.shape[-1])
        scores = jnp.einsum(
            "uqd,ukd->uqk", query_rows, key_flat, preferred_element_type=jnp.float32
        ) / math.sqrt(query_rows.shape[-1])
        list_place = jnp.arange(key_flat.shape[1]) // tile_rows
        valid = (list_place[None, :] < counts[:, None])[:, None, :]
        masked = jnp.where(valid, scores, -jnp.inf)
        peak = jnp.max(masked, axis=-1, keepdims=True)
        weights = jnp.where(valid, jnp.exp(masked - peak), jnp.float32(0.0))
        total = jnp.sum(weights, axis=-1, keepdims=True)
        probs = weights.astype(jnp.bfloat16)
        mixed = (
            jnp.einsum("uqk,ukd->uqd", probs, value_flat, preferred_element_type=jnp.float32)
            / total
        )
        return mixed.astype(jnp.bfloat16)

    grouped = (
        slot_index.reshape(-1, group_size),
        tile_index.reshape(-1, group_size),
        head_index.reshape(-1, group_size),
    )
    result = lax.map(one_group, grouped)
    return result.reshape(-1, result.shape[2], result.shape[3])


def local_general(queries, keys, values, q_gain, k_gain, key_tiles, key_count):
    devices = lax.axis_size("seq")
    my_index = lax.axis_index("seq")
    q_normed = normed(queries, q_gain)
    k_normed = normed(keys, k_gain)
    stacked = (
        jnp.stack([q_normed, k_normed, values])
        .reshape(3, TILE, HEADS, HEAD_DIM)
        .transpose(2, 0, 1, 3)
    )
    targets = jnp.arange(devices)
    per_device = (HEADS + devices - 1) // devices
    total_slots = devices * per_device
    fewest_slots = total_slots // HEADS
    most_units = (devices + fewest_slots - 1) // fewest_slots

    def slot_layout(slot_number):
        head_of = slot_number * HEADS // total_slots
        head_start = (head_of * total_slots + HEADS - 1) // HEADS
        head_end = ((head_of + 1) * total_slots + HEADS - 1) // HEADS
        sharers = head_end - head_start
        within = slot_number - head_start
        return (head_of, within * devices // sharers, (within + 1) * devices // sharers)

    all_slots = jnp.arange(total_slots).reshape(devices, per_device)
    send_heads = slot_layout(all_slots)[0]
    received = lax.all_to_all(stacked[send_heads], "seq", split_axis=0, concat_axis=0, tiled=True)
    own_heads, lower_tile, upper_tile = slot_layout(my_index * per_device + jnp.arange(per_device))
    offsets = jnp.arange(most_units)
    tile_grid = jnp.minimum(lower_tile[:, None] + offsets[None, :], devices - 1)
    slot_grid = jnp.broadcast_to(jnp.arange(per_device)[:, None], tile_grid.shape)
    head_grid = jnp.broadcast_to(own_heads[:, None], tile_grid.shape)
    unit_total = per_device * most_units
    length = (unit_total + group_size - 1) // group_size * group_size
    finished = attend_units(
        received,
        padded(slot_grid.reshape(-1), length),
        padded(tile_grid.reshape(-1), length),
        padded(head_grid.reshape(-1), length),
        key_tiles,
        key_count,
    )[:unit_total]
    finished = finished.reshape(per_device, most_units, TILE, HEAD_DIM)
    position = targets[:, None] - lower_tile[None, :]
    inside = (position >= 0) & (targets[:, None] < upper_tile[None, :])
    gathered = finished[jnp.arange(per_device)[None, :], jnp.clip(position, 0, most_units - 1)]
    outgoing = jnp.where(inside[:, :, None, None], gathered, jnp.zeros_like(gathered))
    returned = lax.all_to_all(outgoing, "seq", split_axis=0, concat_axis=0, tiled=True)
    head_list = jnp.arange(HEADS)
    head_start = (head_list * total_slots + HEADS - 1) // HEADS
    sharers = ((head_list + 1) * total_slots + HEADS - 1) // HEADS - head_start
    owner_slot = head_start + ((my_index + 1) * sharers - 1) // devices
    pieces = returned[owner_slot // per_device, owner_slot % per_device]
    return pieces.transpose(1, 0, 2).reshape(TILE, HEADS * HEAD_DIM)


ALL_VMEM_BYTES = 60 * 1024 * 1024
IN_HBM = pl.BlockSpec(memory_space=pltpu.HBM)
ANYWHERE = pl.BlockSpec(memory_space=pl.ANY)
IN_SMEM = pl.BlockSpec(memory_space=pltpu.SMEM)
IN_VMEM = pl.BlockSpec(memory_space=pltpu.VMEM)
PARAMS = pltpu.CompilerParams(vmem_limit_bytes=ALL_VMEM_BYTES)
LEAVE_ROOM = pltpu.CompilerParams(vmem_limit_bytes=40 * 1024 * 1024)
LOADS = 2


def head_of(pair, core, slot, full):
    return pair * (2 * full + 1) + (full if slot == full else slot + core * (full + 1))


def columns_of(head):
    return slice(head * HEAD_DIM, (head + 1) * HEAD_DIM)


def traced_columns(head):
    return pl.ds(pl.multiple_of(head * HEAD_DIM, HEAD_DIM), HEAD_DIM)


def bf16(*shape):
    return jax.ShapeDtypeStruct(shape, jnp.bfloat16)


def copy_list(sems):
    return sems, []


def start_copy(copies, source, target):
    sems, started = copies
    started.append(pltpu.make_async_copy(source, target, sems.at[len(started)]))
    started[-1].start()
    return started[-1]


def wait_copies(copies):
    for copy in copies[1]:
        copy.wait()


def norm_in_place(rows, gain, loads, gain_load):
    count = TILE // len(loads)
    for part, load in enumerate(loads):
        here = slice(part * count, (part + 1) * count)
        load.wait()
        squares = jnp.zeros((count, HEAD_DIM), jnp.float32)
        for head in range(HEADS):
            block = rows[here, columns_of(head)].astype(jnp.float32)
            squares = squares + block * block
        mean = jnp.sum(squares, axis=-1, keepdims=True) / (HEADS * HEAD_DIM)
        factor = lax.rsqrt(mean + 1e-06)
        if part == 0:
            gain_load.wait()
        for head in range(HEADS):
            block = rows[here, columns_of(head)].astype(jnp.float32)
            scaled = block * factor * gain[columns_of(head)][None, :]
            rows[here, columns_of(head)] = scaled.astype(jnp.bfloat16)


def prepare_kernel(send, queries, keys, values, q_gain, k_gain, scratch):
    q_rows, k_rows, v_rows, q_scale, k_scale, in_sems = scratch
    loading = copy_list(in_sems)

    def load(source, target):
        parts = [pl.ds(i * TILE // LOADS, TILE // LOADS) for i in range(LOADS)]
        return [start_copy(loading, source.at[part], target.at[part]) for part in parts]

    k_scale_load = start_copy(loading, k_gain, k_scale)
    q_scale_load = start_copy(loading, q_gain, q_scale)
    k_loads, v_loads, q_loads = load(keys, k_rows), load(values, v_rows), load(queries, q_rows)
    norm_in_place(k_rows, k_scale, k_loads, k_scale_load)
    send(k_rows, 1)
    for part in v_loads:
        part.wait()
    send(v_rows, 2)
    norm_in_place(q_rows, q_scale, q_loads, q_scale_load)
    send(q_rows, 0)


def prepare_whole_kernel(full, *refs):
    operands, out, scratch, out_sems = refs[:5], refs[5], refs[6:-1], refs[-1]
    copies = copy_list(out_sems)

    def send(rows, tensor):
        for device in range(out.shape[0]):
            for slot in range(full):
                head = head_of(device // 2, device % 2, slot, full)
                target = out.at[device, pl.ds((3 * slot + tensor) * TILE, TILE)]
                start_copy(copies, rows.at[:, pl.ds(head * HEAD_DIM, HEAD_DIM)], target)

    prepare_kernel(send, *operands, scratch)
    wait_copies(copies)


def prepare_shared_kernel(full, pairs, me_ref, *refs):
    operands, outs, scratch, out_sems = refs[:5], refs[5 : 5 + pairs], refs[5 + pairs : -1], refs[-1]
    copies = copy_list(out_sems)

    def send(rows, tensor):
        for partner, out in enumerate(outs):
            head = head_of(jnp.bitwise_xor(me_ref[0] // 2, partner), 0, full, full)
            target = out.at[pl.ds(tensor * TILE, TILE)]
            start_copy(copies, rows.at[:, traced_columns(head)], target)

    prepare_kernel(send, *operands, scratch)
    wait_copies(copies)


def prepare_scratch(queries, q_gain, copies):
    rows = pltpu.VMEM(queries.shape, jnp.bfloat16)
    scale = pltpu.VMEM(q_gain.shape, jnp.float32)
    sems = pltpu.SemaphoreType.DMA
    return [rows, rows, rows, scale, scale, sems((3 * LOADS + 2,)), sems((copies,))]


def prepare_whole(full, devices, *operands):
    return pl.pallas_call(
        functools.partial(prepare_whole_kernel, full),
        name="prepare_whole",
        out_shape=bf16(devices, 3 * full * TILE, HEAD_DIM),
        in_specs=[IN_HBM] * 5,
        out_specs=ANYWHERE,
        scratch_shapes=prepare_scratch(operands[0], operands[3], 3 * full * devices),
        compiler_params=PARAMS,
    )(*operands)


def prepare_shared(full, pairs, me, *operands):
    return pl.pallas_call(
        functools.partial(prepare_shared_kernel, full, pairs),
        name="prepare_shared",
        out_shape=[bf16(3 * TILE, HEAD_DIM)] * pairs,
        in_specs=[IN_SMEM] + [IN_HBM] * 5,
        out_specs=[ANYWHERE] * pairs,
        scratch_shapes=prepare_scratch(operands[0], operands[3], 3 * pairs),
        compiler_params=PARAMS,
    )(me, *operands)


TOGETHER = 2
UNROLL = 4


def key_marks(keys):
    shape = (keys.shape[0], HEAD_DIM)
    tile = lax.broadcasted_iota(jnp.int32, shape, 0) // TILE
    marks = jnp.where(lax.broadcasted_iota(jnp.int32, shape, 1) == tile, 1.0, 0.0)
    return jnp.concatenate([keys, marks.astype(jnp.bfloat16)], axis=1)


def query_masks(queries, mask):
    bit = jnp.minimum(lax.broadcasted_iota(jnp.int32, queries.shape, 1), 31)
    offsets = jnp.where((mask >> bit) & 1 == 1, jnp.float32(0.0), jnp.float32(-1e30))
    return jnp.concatenate([queries, offsets.astype(jnp.bfloat16)], axis=1)


def attend_rows(queries, keys, values, masks):
    tiles = keys.shape[0] // TILE
    marked = [query_masks(tile, mask) for tile, mask in zip(queries, masks)]
    scores = lax.dot_general(
        jnp.concatenate(marked, axis=0),
        keys,
        (((1,), (1,)), ((), ())),
        preferred_element_type=jnp.float32,
    )
    scale = jnp.float32(math.log2(math.e) / math.sqrt(HEAD_DIM))
    probs, totals = [], []
    for i in range(len(masks)):
        rows = slice(i * TILE, (i + 1) * TILE)
        parts = [scores[rows, tile * TILE : (tile + 1) * TILE] for tile in range(tiles)]
        peak = jnp.max(functools.reduce(jnp.maximum, parts), axis=-1, keepdims=True)
        weights = [jnp.exp2((part - peak) * scale) for part in parts]
        totals.append(jnp.sum(functools.reduce(jnp.add, weights), axis=-1, keepdims=True))
        probs.append(jnp.concatenate([w.astype(jnp.bfloat16) for w in weights], axis=1))
    mixed = jnp.dot(jnp.concatenate(probs, axis=0), values, preferred_element_type=jnp.float32)
    return [
        (mixed[i * TILE : (i + 1) * TILE] / total).astype(jnp.bfloat16)
        for i, total in enumerate(totals)
    ]


def attend_slot(mask_ref, slot, here, first, out, out_first, stride, marked):
    def part(tile, tensor):
        return here[tile, first + tensor * TILE : first + (tensor + 1) * TILE]

    marked[...] = key_marks(part(slice(None), 1).reshape(-1, HEAD_DIM))

    def step(index, carry):
        for product in range(UNROLL):
            at = (index * UNROLL + product) * TOGETHER
            tiles = [(at + i) * stride for i in range(TOGETHER)]
            values = part(slice(None), 2).reshape(-1, HEAD_DIM)
            masks = [mask_ref[slot, tile] for tile in tiles]
            blocks = attend_rows([part(tile, 0) for tile in tiles], marked[...], values, masks)
            for tile, block in zip(tiles, blocks):
                out[tile, out_first : out_first + TILE] = block
        return carry

    lax.fori_loop(0, here.shape[0] // (stride * TOGETHER * UNROLL), step, 0)


def marked_keys(devices):
    return pltpu.VMEM((devices * TILE, 2 * HEAD_DIM), jnp.bfloat16)


def attend_whole_kernel(full, mask_ref, here, out, marked):
    for slot in range(full):
        attend_slot(mask_ref, slot, here, 3 * slot * TILE, out, slot * TILE, 1, marked)


def attend_whole(full, masks, here):
    return pl.pallas_call(
        functools.partial(attend_whole_kernel, full),
        name="attend_whole",
        out_shape=bf16(here.shape[0], full * TILE, HEAD_DIM),
        in_specs=[IN_SMEM, IN_VMEM],
        out_specs=IN_VMEM,
        scratch_shapes=[marked_keys(here.shape[0])],
        compiler_params=LEAVE_ROOM,
    )(masks, here)


def attend_shared_kernel(full, pairs, mask_ref, *refs):
    blocks, other, outs = refs[:pairs], refs[pairs], refs[pairs + 1 : 2 * pairs + 1]
    here, out, marked, in_sems, out_sems = refs[2 * pairs + 1 :]
    loads, stores = copy_list(in_sems), copy_list(out_sems)
    for partner, block in enumerate(blocks):
        start_copy(loads, block, here.at[2 * partner])
        start_copy(loads, other.at[partner], here.at[2 * partner + 1, pl.ds(TILE, 2 * TILE)])
    wait_copies(loads)
    attend_slot(mask_ref, full, here, 0, out, 0, 2, marked)
    for partner, target in enumerate(outs):
        start_copy(stores, out.at[2 * partner], target)
    wait_copies(stores)


def attend_shared(full, masks, blocks, other):
    pairs = len(blocks)
    return pl.pallas_call(
        functools.partial(attend_shared_kernel, full, pairs),
        name="attend_shared",
        out_shape=[bf16(TILE, HEAD_DIM)] * pairs,
        in_specs=[IN_SMEM] + [ANYWHERE] * (pairs + 1),
        out_specs=[ANYWHERE] * pairs,
        scratch_shapes=[
            pltpu.VMEM((2 * pairs, 3 * TILE, HEAD_DIM), jnp.bfloat16),
            pltpu.VMEM((2 * pairs, TILE, HEAD_DIM), jnp.bfloat16),
            marked_keys(2 * pairs),
            pltpu.SemaphoreType.DMA((2 * pairs,)),
            pltpu.SemaphoreType.DMA((pairs,)),
        ],
        compiler_params=PARAMS,
    )(masks, *blocks, other)


def join_kernel(*refs):
    blocks, (out, rows, in_sems, out_sems) = refs[:-4], refs[-4:]
    loads, stores = copy_list(in_sems), copy_list(out_sems)
    for index, block in enumerate(blocks):
        start_copy(loads, block.at[pl.ds(TILE, 2 * TILE)], rows.at[index])
    for index, load in enumerate(loads[1]):
        load.wait()
        start_copy(stores, rows.at[index], out.at[index])
    wait_copies(stores)


def join_keys_values(blocks):
    shape = (len(blocks), 2 * TILE, HEAD_DIM)
    sems = pltpu.SemaphoreType.DMA((len(blocks),))
    return pl.pallas_call(
        join_kernel,
        name="join_keys_values",
        out_shape=bf16(*shape),
        in_specs=[ANYWHERE] * len(blocks),
        out_specs=ANYWHERE,
        scratch_shapes=[pltpu.VMEM(shape, jnp.bfloat16), sems, sems],
        compiler_params=PARAMS,
    )(*blocks)


def collect_shared_kernel(full, me_ref, *refs):
    blocks, (out, rows, in_sems, out_sems) = refs[:-4], refs[-4:]
    loads, stores = copy_list(in_sems), copy_list(out_sems)
    for partner, block in enumerate(blocks):
        start_copy(loads, block, rows.at[partner])
    for partner, load in enumerate(loads[1]):
        load.wait()
        head = head_of(jnp.bitwise_xor(me_ref[0] // 2, partner), 0, full, full)
        start_copy(stores, rows.at[partner], out.at[:, traced_columns(head)])
    wait_copies(stores)


def collect_shared(full, shape, me, blocks):
    sems = pltpu.SemaphoreType.DMA((len(blocks),))
    return pl.pallas_call(
        functools.partial(collect_shared_kernel, full),
        name="collect_shared",
        out_shape=bf16(*shape),
        in_specs=[IN_SMEM] + [ANYWHERE] * len(blocks),
        out_specs=IN_HBM,
        scratch_shapes=[pltpu.VMEM((len(blocks), TILE, HEAD_DIM), jnp.bfloat16), sems, sems],
        compiler_params=PARAMS,
    )(me, *blocks)


def collect_whole_kernel(full, here, _, out, sems):
    stores = copy_list(sems)
    for device in range(here.shape[0]):
        for slot in range(full):
            head = head_of(device // 2, device % 2, slot, full)
            target = out.at[:, pl.ds(head * HEAD_DIM, HEAD_DIM)]
            start_copy(stores, here.at[device, pl.ds(slot * TILE, TILE)], target)
    wait_copies(stores)


def collect_whole(full, here, so_far):
    return pl.pallas_call(
        functools.partial(collect_whole_kernel, full),
        name="collect_whole",
        out_shape=bf16(*so_far.shape),
        in_specs=[IN_VMEM, IN_HBM],
        out_specs=IN_HBM,
        scratch_shapes=[pltpu.SemaphoreType.DMA((full * here.shape[0],))],
        input_output_aliases={1: 0},
        compiler_params=LEAVE_ROOM,
    )(here, so_far)


def with_all(blocks):
    return lax.all_to_all(blocks, "seq", split_axis=0, concat_axis=0, tiled=True)


def with_partner(block, k):
    devices = lax.axis_size("seq")
    return lax.ppermute(block, "seq", [(i, i ^ (2 * k)) for i in range(devices)]) if k else block


def with_sibling(block):
    return lax.ppermute(block, "seq", [(i, i ^ 1) for i in range(lax.axis_size("seq"))])


def after(value, *others):
    return lax.optimization_barrier((value, *others))[0]


def all_after(values, *others):
    return list(lax.optimization_barrier((*values, *others))[: len(values)])


def tile_masks(full, my_index, key_tiles, key_count):
    slots = jnp.arange(full + 1)
    within = jnp.where(slots < full, slots + my_index % 2 * (full + 1), full)
    heads = my_index // 2 * (2 * full + 1) + within
    tiles, counts = key_tiles[heads], key_count[heads]
    flip = jnp.where(slots < full, 0, my_index)
    bits = jnp.left_shift(1, jnp.bitwise_xor(tiles, flip[:, None, None]))
    allowed = jnp.arange(tiles.shape[-1]) < counts[:, :, None]
    masks = jnp.sum(jnp.where(allowed, bits, 0), axis=-1)
    order = jnp.bitwise_xor(jnp.arange(tiles.shape[1])[None, :], flip[:, None])
    return jnp.take_along_axis(masks, order, axis=1)


def local_paired(queries, keys, values, q_gain, k_gain, key_tiles, key_count):
    devices = lax.axis_size("seq")
    pairs = devices // 2
    full = HEADS // devices
    my_index = lax.axis_index("seq")
    me = my_index.reshape(1)
    rest = (keys, values, q_gain, k_gain)

    whole = prepare_whole(full, devices, queries, *rest)
    masks = tile_masks(full, my_index, key_tiles, key_count)
    shared = prepare_shared(full, pairs, me, after(queries, masks, whole), *rest)
    whole = with_all(whole)
    shared = [with_partner(block, k) for k, block in enumerate(shared)]
    near, far = shared[: pairs // 2], shared[pairs // 2 :]
    whole_out = attend_whole(full, masks, after(whole, *near))
    shared = all_after(near + far, whole_out)
    whole_back = with_all(after(whole_out, *shared))
    other = with_sibling(join_keys_values(shared))
    shared_out = attend_shared(full, masks, shared, other)
    shared_back = [with_partner(block, k) for k, block in enumerate(shared_out)]
    so_far = collect_shared(full, queries.shape, me, shared_back)
    return collect_whole(full, whole_back, so_far)


def paired_fits(mesh, key_tiles_shape):
    devices = mesh.shape["seq"]
    per_pair, rest = divmod(2 * HEADS, devices)
    return (
        rest == 0
        and per_pair % 2 == 1
        and per_pair >= 3
        and devices >= 16
        and devices & (devices - 1) == 0
        and key_tiles_shape[1] == devices
        and devices <= 31
    )


def solution(mesh):
    in_specs = (
        P(("groups", "seq"), None),
        P(("groups", "seq"), None),
        P(("groups", "seq"), None),
        P(),
        P(),
        P(),
        P(),
    )
    out_specs = P(("groups", "seq"), None)

    def run(*operands):
        paired = paired_fits(mesh, operands[5].shape)
        body = local_paired if paired else local_general
        return jax.shard_map(
            body, mesh=mesh, in_specs=in_specs, out_specs=out_specs, check_vma=False
        )(*operands)

    return run
```

```python
import functools
import math

import jax
import jax.numpy as jnp
from jax import lax
from jax.experimental import pallas as pl
from jax.experimental.pallas import tpu as pltpu
from jax.sharding import PartitionSpec as P

HEADS = 40
HEAD_DIM = 128
TILE = 128


group_size = 4


def normed(rows, gain):
    values32 = rows.astype(jnp.float32)
    factor = lax.rsqrt(jnp.mean(values32 * values32, axis=-1, keepdims=True) + 1e-06)
    return (values32 * factor * gain).astype(jnp.bfloat16)


def padded(entries, length):
    return jnp.pad(entries, (0, length - entries.shape[0]), mode="edge")


def attend_units(received, slot_index, tile_index, head_index, key_tiles, key_count):

    def one_group(unit_items):
        slot_part, tile_part, head_part = unit_items
        query_rows = received[tile_part, slot_part, 0]
        key_lists = key_tiles[head_part, tile_part]
        counts = key_count[head_part, tile_part]
        key_block = received[key_lists, slot_part[:, None], 1]
        value_block = received[key_lists, slot_part[:, None], 2]
        units = query_rows.shape[0]
        tile_rows = query_rows.shape[1]
        key_flat = key_block.reshape(units, -1, key_block.shape[-1])
        value_flat = value_block.reshape(units, -1, value_block.shape[-1])
        scores = jnp.einsum(
            "uqd,ukd->uqk", query_rows, key_flat, preferred_element_type=jnp.float32
        ) / math.sqrt(query_rows.shape[-1])
        list_place = jnp.arange(key_flat.shape[1]) // tile_rows
        valid = (list_place[None, :] < counts[:, None])[:, None, :]
        masked = jnp.where(valid, scores, -jnp.inf)
        peak = jnp.max(masked, axis=-1, keepdims=True)
        weights = jnp.where(valid, jnp.exp(masked - peak), jnp.float32(0.0))
        total = jnp.sum(weights, axis=-1, keepdims=True)
        probs = weights.astype(jnp.bfloat16)
        mixed = (
            jnp.einsum("uqk,ukd->uqd", probs, value_flat, preferred_element_type=jnp.float32)
            / total
        )
        return mixed.astype(jnp.bfloat16)

    grouped = (
        slot_index.reshape(-1, group_size),
        tile_index.reshape(-1, group_size),
        head_index.reshape(-1, group_size),
    )
    result = lax.map(one_group, grouped)
    return result.reshape(-1, result.shape[2], result.shape[3])


def local_general(queries, keys, values, q_gain, k_gain, key_tiles, key_count):
    devices = lax.axis_size("seq")
    my_index = lax.axis_index("seq")
    q_normed = normed(queries, q_gain)
    k_normed = normed(keys, k_gain)
    stacked = (
        jnp.stack([q_normed, k_normed, values])
        .reshape(3, TILE, HEADS, HEAD_DIM)
        .transpose(2, 0, 1, 3)
    )
    targets = jnp.arange(devices)
    per_device = (HEADS + devices - 1) // devices
    total_slots = devices * per_device
    fewest_slots = total_slots // HEADS
    most_units = (devices + fewest_slots - 1) // fewest_slots

    def slot_layout(slot_number):
        head_of = slot_number * HEADS // total_slots
        head_start = (head_of * total_slots + HEADS - 1) // HEADS
        head_end = ((head_of + 1) * total_slots + HEADS - 1) // HEADS
        sharers = head_end - head_start
        within = slot_number - head_start
        return (head_of, within * devices // sharers, (within + 1) * devices // sharers)

    all_slots = jnp.arange(total_slots).reshape(devices, per_device)
    send_heads = slot_layout(all_slots)[0]
    received = lax.all_to_all(stacked[send_heads], "seq", split_axis=0, concat_axis=0, tiled=True)
    own_heads, lower_tile, upper_tile = slot_layout(my_index * per_device + jnp.arange(per_device))
    offsets = jnp.arange(most_units)
    tile_grid = jnp.minimum(lower_tile[:, None] + offsets[None, :], devices - 1)
    slot_grid = jnp.broadcast_to(jnp.arange(per_device)[:, None], tile_grid.shape)
    head_grid = jnp.broadcast_to(own_heads[:, None], tile_grid.shape)
    unit_total = per_device * most_units
    length = (unit_total + group_size - 1) // group_size * group_size
    finished = attend_units(
        received,
        padded(slot_grid.reshape(-1), length),
        padded(tile_grid.reshape(-1), length),
        padded(head_grid.reshape(-1), length),
        key_tiles,
        key_count,
    )[:unit_total]
    finished = finished.reshape(per_device, most_units, TILE, HEAD_DIM)
    position = targets[:, None] - lower_tile[None, :]
    inside = (position >= 0) & (targets[:, None] < upper_tile[None, :])
    gathered = finished[jnp.arange(per_device)[None, :], jnp.clip(position, 0, most_units - 1)]
    outgoing = jnp.where(inside[:, :, None, None], gathered, jnp.zeros_like(gathered))
    returned = lax.all_to_all(outgoing, "seq", split_axis=0, concat_axis=0, tiled=True)
    head_list = jnp.arange(HEADS)
    head_start = (head_list * total_slots + HEADS - 1) // HEADS
    sharers = ((head_list + 1) * total_slots + HEADS - 1) // HEADS - head_start
    owner_slot = head_start + ((my_index + 1) * sharers - 1) // devices
    pieces = returned[owner_slot // per_device, owner_slot % per_device]
    return pieces.transpose(1, 0, 2).reshape(TILE, HEADS * HEAD_DIM)


ALL_VMEM_BYTES = 60 * 1024 * 1024
IN_HBM = pl.BlockSpec(memory_space=pltpu.HBM)
ANYWHERE = pl.BlockSpec(memory_space=pl.ANY)
IN_SMEM = pl.BlockSpec(memory_space=pltpu.SMEM)
IN_VMEM = pl.BlockSpec(memory_space=pltpu.VMEM)
PARAMS = pltpu.CompilerParams(vmem_limit_bytes=ALL_VMEM_BYTES)
LEAVE_ROOM = pltpu.CompilerParams(vmem_limit_bytes=40 * 1024 * 1024)
LOADS = 2


def head_of(pair, core, slot, full):
    return pair * (2 * full + 1) + (full if slot == full else slot + core * (full + 1))


def columns_of(head):
    return slice(head * HEAD_DIM, (head + 1) * HEAD_DIM)


def traced_columns(head):
    return pl.ds(pl.multiple_of(head * HEAD_DIM, HEAD_DIM), HEAD_DIM)


def bf16(*shape):
    return jax.ShapeDtypeStruct(shape, jnp.bfloat16)


def copy_list(sems):
    return sems, []


def start_copy(copies, source, target):
    sems, started = copies
    started.append(pltpu.make_async_copy(source, target, sems.at[len(started)]))
    started[-1].start()
    return started[-1]


def wait_copies(copies):
    for copy in copies[1]:
        copy.wait()


def norm_in_place(rows, gain, loads, gain_load):
    count = TILE // len(loads)
    for part, load in enumerate(loads):
        here = slice(part * count, (part + 1) * count)
        load.wait()
        squares = jnp.zeros((count, HEAD_DIM), jnp.float32)
        for head in range(HEADS):
            block = rows[here, columns_of(head)].astype(jnp.float32)
            squares = squares + block * block
        mean = jnp.sum(squares, axis=-1, keepdims=True) / (HEADS * HEAD_DIM)
        factor = lax.rsqrt(mean + 1e-06)
        if part == 0:
            gain_load.wait()
        for head in range(HEADS):
            block = rows[here, columns_of(head)].astype(jnp.float32)
            scaled = block * factor * gain[columns_of(head)][None, :]
            rows[here, columns_of(head)] = scaled.astype(jnp.bfloat16)


def prepare_kernel(send, queries, keys, values, q_gain, k_gain, scratch):
    q_rows, k_rows, v_rows, q_scale, k_scale, in_sems = scratch
    loading = copy_list(in_sems)

    def load(source, target):
        parts = [pl.ds(i * TILE // LOADS, TILE // LOADS) for i in range(LOADS)]
        return [start_copy(loading, source.at[part], target.at[part]) for part in parts]

    k_scale_load = start_copy(loading, k_gain, k_scale)
    q_scale_load = start_copy(loading, q_gain, q_scale)
    k_loads, v_loads, q_loads = load(keys, k_rows), load(values, v_rows), load(queries, q_rows)
    norm_in_place(k_rows, k_scale, k_loads, k_scale_load)
    send(k_rows, 1)
    for part in v_loads:
        part.wait()
    send(v_rows, 2)
    norm_in_place(q_rows, q_scale, q_loads, q_scale_load)
    send(q_rows, 0)


def prepare_whole_kernel(full, *refs):
    operands, out, scratch, out_sems = refs[:5], refs[5], refs[6:-1], refs[-1]
    copies = copy_list(out_sems)

    def send(rows, tensor):
        for device in range(out.shape[0]):
            for slot in range(full):
                head = head_of(device // 2, device % 2, slot, full)
                target = out.at[device, pl.ds((3 * slot + tensor) * TILE, TILE)]
                start_copy(copies, rows.at[:, pl.ds(head * HEAD_DIM, HEAD_DIM)], target)

    prepare_kernel(send, *operands, scratch)
    wait_copies(copies)


def prepare_shared_kernel(full, me_ref, *refs):
    operands, outs, scratch, out_sems = refs[:5], refs[5:7], refs[7:-1], refs[-1]
    copies = copy_list(out_sems)

    def send(rows, tensor):
        for odd, out in enumerate(outs):
            for flip in range(out.shape[0]):
                pair = jnp.bitwise_xor(me_ref[0] // 2, 2 * flip + odd)
                target = out.at[flip, pl.ds(tensor * TILE, TILE)]
                source = rows.at[:, traced_columns(head_of(pair, 0, full, full))]
                start_copy(copies, source, target)

    prepare_kernel(send, *operands, scratch)
    wait_copies(copies)


def prepare_scratch(queries, q_gain, copies):
    rows = pltpu.VMEM(queries.shape, jnp.bfloat16)
    scale = pltpu.VMEM(q_gain.shape, jnp.float32)
    sems = pltpu.SemaphoreType.DMA
    return [rows, rows, rows, scale, scale, sems((3 * LOADS + 2,)), sems((copies,))]


def prepare_whole(full, devices, *operands):
    return pl.pallas_call(
        functools.partial(prepare_whole_kernel, full),
        name="prepare_whole",
        out_shape=bf16(devices, 3 * full * TILE, HEAD_DIM),
        in_specs=[IN_HBM] * 5,
        out_specs=ANYWHERE,
        scratch_shapes=prepare_scratch(operands[0], operands[3], 3 * full * devices),
        compiler_params=PARAMS,
    )(*operands)


def prepare_shared(full, pairs, me, *operands):
    return pl.pallas_call(
        functools.partial(prepare_shared_kernel, full),
        name="prepare_shared",
        out_shape=[bf16(pairs // 2, 3 * TILE, HEAD_DIM)] * 2,
        in_specs=[IN_SMEM] + [IN_HBM] * 5,
        out_specs=[ANYWHERE] * 2,
        scratch_shapes=prepare_scratch(operands[0], operands[3], 3 * pairs),
        compiler_params=PARAMS,
    )(me, *operands)


def join_columns_kernel(own, other, *refs):
    outs, (rows, in_sems, out_sems) = refs[:-3], refs[-3:]
    count = own.shape[1]
    loads, stores = copy_list(in_sems), copy_list(out_sems)
    for flip in range(len(outs)):
        start_copy(loads, own.at[flip], rows.at[flip, pl.ds(0, count)])
        start_copy(loads, other.at[flip], rows.at[flip, pl.ds(count, count)])
    for flip, out in enumerate(outs):
        loads[1][2 * flip].wait()
        loads[1][2 * flip + 1].wait()
        start_copy(stores, rows.at[flip], out)
    wait_copies(stores)


def join_columns(own, other):
    flips, count = own.shape[:2]
    return pl.pallas_call(
        join_columns_kernel,
        name="join_columns",
        out_shape=[bf16(2 * count, HEAD_DIM)] * flips,
        in_specs=[ANYWHERE] * 2,
        out_specs=[ANYWHERE] * flips,
        scratch_shapes=[
            pltpu.VMEM((flips, 2 * count, HEAD_DIM), jnp.bfloat16),
            pltpu.SemaphoreType.DMA((2 * flips,)),
            pltpu.SemaphoreType.DMA((flips,)),
        ],
        compiler_params=LEAVE_ROOM,
    )(own, other)


TOGETHER = 2
UNROLL = 8


def key_marks(keys):
    shape = (keys.shape[0], HEAD_DIM)
    tile = lax.broadcasted_iota(jnp.int32, shape, 0) // TILE
    marks = jnp.where(lax.broadcasted_iota(jnp.int32, shape, 1) == tile, 1.0, 0.0)
    return jnp.concatenate([keys, marks.astype(jnp.bfloat16)], axis=1)


def query_masks(queries, mask):
    bit = jnp.minimum(lax.broadcasted_iota(jnp.int32, queries.shape, 1), 31)
    offsets = jnp.where((mask >> bit) & 1 == 1, jnp.float32(0.0), jnp.float32(-1e30))
    return jnp.concatenate([queries, offsets.astype(jnp.bfloat16)], axis=1)


def attend_rows(queries, keys, values, masks):
    tiles = keys.shape[0] // TILE
    marked = [query_masks(tile, mask) for tile, mask in zip(queries, masks)]
    scores = lax.dot_general(
        jnp.concatenate(marked, axis=0),
        keys,
        (((1,), (1,)), ((), ())),
        preferred_element_type=jnp.float32,
    )
    scale = jnp.float32(math.log2(math.e) / math.sqrt(HEAD_DIM))
    probs, totals = [], []
    for i in range(len(masks)):
        rows = slice(i * TILE, (i + 1) * TILE)
        parts = [scores[rows, tile * TILE : (tile + 1) * TILE] for tile in range(tiles)]
        peak = jnp.max(functools.reduce(jnp.maximum, parts), axis=-1, keepdims=True)
        weights = [jnp.exp2((part - peak) * scale) for part in parts]
        totals.append(jnp.sum(functools.reduce(jnp.add, weights), axis=-1, keepdims=True))
        probs.append(jnp.concatenate([w.astype(jnp.bfloat16) for w in weights], axis=1))
    mixed = jnp.dot(jnp.concatenate(probs, axis=0), values, preferred_element_type=jnp.float32)
    return [
        (mixed[i * TILE : (i + 1) * TILE] / total).astype(jnp.bfloat16)
        for i, total in enumerate(totals)
    ]


def attend_slot(mask_ref, slot, here, first, out, out_first, stride, marked):
    def part(tile, tensor):
        return here[tile, first + tensor * TILE : first + (tensor + 1) * TILE]

    marked[...] = key_marks(part(slice(None), 1).reshape(-1, HEAD_DIM))

    products = here.shape[0] // (stride * TOGETHER)
    unroll = math.gcd(products, UNROLL)

    def step(index, carry):
        for product in range(unroll):
            at = (index * unroll + product) * TOGETHER
            tiles = [(at + i) * stride for i in range(TOGETHER)]
            values = part(slice(None), 2).reshape(-1, HEAD_DIM)
            masks = [mask_ref[slot, tile] for tile in tiles]
            blocks = attend_rows([part(tile, 0) for tile in tiles], marked[...], values, masks)
            for tile, block in zip(tiles, blocks):
                out[tile, out_first : out_first + TILE] = block
        return carry

    lax.fori_loop(0, products // unroll, step, 0)


def marked_keys(devices):
    return pltpu.VMEM((devices * TILE, 2 * HEAD_DIM), jnp.bfloat16)


def attend_whole_kernel(full, mask_ref, here, outs, out, marked, sems):
    stores = copy_list(sems)
    for slot in range(full):
        attend_slot(mask_ref, slot, here, 3 * slot * TILE, out, slot * TILE, 1, marked)
        rows = pl.ds(slot * TILE, TILE)
        start_copy(stores, out.at[:, rows], outs.at[:, rows])
    wait_copies(stores)


def attend_whole(full, masks, here):
    shape = (here.shape[0], full * TILE, HEAD_DIM)
    return pl.pallas_call(
        functools.partial(attend_whole_kernel, full),
        name="attend_whole",
        out_shape=bf16(*shape),
        in_specs=[IN_SMEM, IN_VMEM],
        out_specs=IN_HBM,
        scratch_shapes=[
            pltpu.VMEM(shape, jnp.bfloat16),
            marked_keys(here.shape[0]),
            pltpu.SemaphoreType.DMA((full,)),
        ],
        compiler_params=LEAVE_ROOM,
    )(masks, here)


def attend_shared_kernel(full, mask_ref, *refs):
    blocks, (other, *outs), scratch = refs[:-8], refs[-8:-5], refs[-5:]
    here, out, marked, in_sems, out_sems = scratch
    loads, stores = copy_list(in_sems), copy_list(out_sems)
    for flip, block in enumerate(blocks):
        for odd in range(2):
            partner = 2 * flip + odd
            start_copy(loads, block.at[pl.ds(3 * odd * TILE, 3 * TILE)], here.at[2 * partner])
            target = here.at[2 * partner + 1, pl.ds(TILE, 2 * TILE)]
            start_copy(loads, other.at[partner], target)
    wait_copies(loads)
    attend_slot(mask_ref, full, here, 0, out, 0, 2, marked)
    for flip in range(len(blocks)):
        for odd in range(2):
            start_copy(stores, out.at[2 * (2 * flip + odd)], outs[odd].at[flip])
    wait_copies(stores)


def attend_shared(full, masks, blocks, other):
    flips = len(blocks)
    return pl.pallas_call(
        functools.partial(attend_shared_kernel, full),
        name="attend_shared",
        out_shape=[bf16(flips, TILE, HEAD_DIM)] * 2,
        in_specs=[IN_SMEM] + [ANYWHERE] * (flips + 1),
        out_specs=[ANYWHERE] * 2,
        scratch_shapes=[
            pltpu.VMEM((4 * flips, 3 * TILE, HEAD_DIM), jnp.bfloat16),
            pltpu.VMEM((4 * flips, TILE, HEAD_DIM), jnp.bfloat16),
            marked_keys(4 * flips),
            pltpu.SemaphoreType.DMA((4 * flips,)),
            pltpu.SemaphoreType.DMA((2 * flips,)),
        ],
        compiler_params=LEAVE_ROOM,
    )(masks, *blocks, other)


def join_keys_values_kernel(*refs):
    blocks, (out, rows, in_sems, out_sems) = refs[:-4], refs[-4:]
    loads, stores = copy_list(in_sems), copy_list(out_sems)
    for partner in range(2 * len(blocks)):
        source = blocks[partner // 2].at[pl.ds((3 * (partner % 2) + 1) * TILE, 2 * TILE)]
        start_copy(loads, source, rows.at[partner])
    for partner, load in enumerate(loads[1]):
        load.wait()
        start_copy(stores, rows.at[partner], out.at[partner])
    wait_copies(stores)


def join_keys_values(blocks):
    shape = (2 * len(blocks), 2 * TILE, HEAD_DIM)
    sems = pltpu.SemaphoreType.DMA((2 * len(blocks),))
    return pl.pallas_call(
        join_keys_values_kernel,
        name="join_keys_values",
        out_shape=bf16(*shape),
        in_specs=[ANYWHERE] * len(blocks),
        out_specs=ANYWHERE,
        scratch_shapes=[pltpu.VMEM(shape, jnp.bfloat16), sems, sems],
        compiler_params=LEAVE_ROOM,
    )(*blocks)


def collect_shared_kernel(full, me_ref, *refs):
    blocks, (out, rows, in_sems, out_sems) = refs[:-4], refs[-4:]
    loads, stores = copy_list(in_sems), copy_list(out_sems)
    for flip, block in enumerate(blocks):
        start_copy(loads, block, rows.at[flip])
    for flip, load in enumerate(loads[1]):
        load.wait()
        for odd in range(2):
            pair = jnp.bitwise_xor(me_ref[0] // 2, 2 * flip + odd)
            target = out.at[:, traced_columns(head_of(pair, 0, full, full))]
            start_copy(stores, rows.at[flip, pl.ds(odd * TILE, TILE)], target)
    wait_copies(stores)


def collect_shared(full, shape, me, blocks):
    flips = len(blocks)
    return pl.pallas_call(
        functools.partial(collect_shared_kernel, full),
        name="collect_shared",
        out_shape=bf16(*shape),
        in_specs=[IN_SMEM] + [ANYWHERE] * flips,
        out_specs=IN_HBM,
        scratch_shapes=[
            pltpu.VMEM((flips, 2 * TILE, HEAD_DIM), jnp.bfloat16),
            pltpu.SemaphoreType.DMA((flips,)),
            pltpu.SemaphoreType.DMA((2 * flips,)),
        ],
        compiler_params=LEAVE_ROOM,
    )(me, *blocks)


def collect_whole_kernel(full, here, _, out, sems):
    stores = copy_list(sems)
    for device in range(here.shape[0]):
        for slot in range(full):
            head = head_of(device // 2, device % 2, slot, full)
            target = out.at[:, pl.ds(head * HEAD_DIM, HEAD_DIM)]
            start_copy(stores, here.at[device, pl.ds(slot * TILE, TILE)], target)
    wait_copies(stores)


def collect_whole(full, here, so_far):
    return pl.pallas_call(
        functools.partial(collect_whole_kernel, full),
        name="collect_whole",
        out_shape=bf16(*so_far.shape),
        in_specs=[IN_VMEM, IN_HBM],
        out_specs=IN_HBM,
        scratch_shapes=[pltpu.SemaphoreType.DMA((full * here.shape[0],))],
        input_output_aliases={1: 0},
        compiler_params=LEAVE_ROOM,
    )(here, so_far)


def with_all(blocks):
    return lax.all_to_all(blocks, "seq", split_axis=0, concat_axis=0, tiled=True)


def with_partner(block, k):
    devices = lax.axis_size("seq")
    return lax.ppermute(block, "seq", [(i, i ^ (2 * k)) for i in range(devices)]) if k else block


def with_sibling(block):
    return lax.ppermute(block, "seq", [(i, i ^ 1) for i in range(lax.axis_size("seq"))])


def after(value, *others):
    return lax.optimization_barrier((value, *others))[0]


def all_after(values, *others):
    return list(lax.optimization_barrier((*values, *others))[: len(values)])


def tile_masks(full, my_index, key_tiles, key_count):
    slots = jnp.arange(full + 1)
    within = jnp.where(slots < full, slots + my_index % 2 * (full + 1), full)
    heads = my_index // 2 * (2 * full + 1) + within
    tiles, counts = key_tiles[heads], key_count[heads]
    flip = jnp.where(slots < full, 0, my_index)
    bits = jnp.left_shift(1, jnp.bitwise_xor(tiles, flip[:, None, None]))
    allowed = jnp.arange(tiles.shape[-1]) < counts[:, :, None]
    masks = jnp.sum(jnp.where(allowed, bits, 0), axis=-1)
    order = jnp.bitwise_xor(jnp.arange(tiles.shape[1])[None, :], flip[:, None])
    return jnp.take_along_axis(masks, order, axis=1)


def local_paired(queries, keys, values, q_gain, k_gain, key_tiles, key_count):
    devices = lax.axis_size("seq")
    pairs = devices // 2
    full = HEADS // devices
    my_index = lax.axis_index("seq")
    me = my_index.reshape(1)
    rest = (keys, values, q_gain, k_gain)

    whole = prepare_whole(full, devices, queries, *rest)
    masks = tile_masks(full, my_index, key_tiles, key_count)
    even, odd = prepare_shared(full, pairs, me, after(queries, masks, whole), *rest)
    whole = with_all(whole)
    shared = join_columns(even, with_partner(odd, 1))
    near, far = shared[: pairs // 4], shared[pairs // 4 :]
    near = [with_partner(block, 2 * flip) for flip, block in enumerate(near)]
    whole = after(whole, *near, *far)
    far = all_after(far, whole)
    far = [with_partner(block, 2 * flip + pairs // 2) for flip, block in enumerate(far)]
    whole_out = attend_whole(full, masks, whole)
    shared = all_after(near + far, whole_out)
    whole_back = with_all(after(whole_out, *shared))
    other = with_sibling(join_keys_values(shared))
    even, odd = attend_shared(full, masks, shared, other)
    shared_back = join_columns(even, with_partner(odd, 1))
    shared_back = [with_partner(block, 2 * flip) for flip, block in enumerate(shared_back)]
    so_far = collect_shared(full, queries.shape, me, shared_back)
    return collect_whole(full, whole_back, so_far)


def paired_fits(mesh, key_tiles_shape):
    devices = mesh.shape["seq"]
    per_pair, rest = divmod(2 * HEADS, devices)
    return (
        rest == 0
        and per_pair % 2 == 1
        and per_pair >= 3
        and devices >= 16
        and devices & (devices - 1) == 0
        and key_tiles_shape[1] == devices
        and devices <= 31
    )


def solution(mesh):
    in_specs = (
        P(("groups", "seq"), None),
        P(("groups", "seq"), None),
        P(("groups", "seq"), None),
        P(),
        P(),
        P(),
        P(),
    )
    out_specs = P(("groups", "seq"), None)

    def run(*operands):
        paired = paired_fits(mesh, operands[5].shape)
        body = local_paired if paired else local_general
        return jax.shard_map(
            body, mesh=mesh, in_specs=in_specs, out_specs=out_specs, check_vma=False
        )(*operands)

    return run
```

```python
import functools
import math

import jax
import jax.numpy as jnp
from jax import lax
from jax.experimental import pallas as pl
from jax.experimental.pallas import tpu as pltpu
from jax.sharding import PartitionSpec as P

HEADS = 40
HEAD_DIM = 128
TILE = 128


group_size = 4


def normed(rows, gain):
    values32 = rows.astype(jnp.float32)
    factor = lax.rsqrt(jnp.mean(values32 * values32, axis=-1, keepdims=True) + 1e-06)
    return (values32 * factor * gain).astype(jnp.bfloat16)


def padded(entries, length):
    return jnp.pad(entries, (0, length - entries.shape[0]), mode="edge")


def attend_units(received, slot_index, tile_index, head_index, key_tiles, key_count):

    def one_group(unit_items):
        slot_part, tile_part, head_part = unit_items
        query_rows = received[tile_part, slot_part, 0]
        key_lists = key_tiles[head_part, tile_part]
        counts = key_count[head_part, tile_part]
        key_block = received[key_lists, slot_part[:, None], 1]
        value_block = received[key_lists, slot_part[:, None], 2]
        units = query_rows.shape[0]
        tile_rows = query_rows.shape[1]
        key_flat = key_block.reshape(units, -1, key_block.shape[-1])
        value_flat = value_block.reshape(units, -1, value_block.shape[-1])
        scores = jnp.einsum(
            "uqd,ukd->uqk", query_rows, key_flat, preferred_element_type=jnp.float32
        ) / math.sqrt(query_rows.shape[-1])
        list_place = jnp.arange(key_flat.shape[1]) // tile_rows
        valid = (list_place[None, :] < counts[:, None])[:, None, :]
        masked = jnp.where(valid, scores, -jnp.inf)
        peak = jnp.max(masked, axis=-1, keepdims=True)
        weights = jnp.where(valid, jnp.exp(masked - peak), jnp.float32(0.0))
        total = jnp.sum(weights, axis=-1, keepdims=True)
        probs = weights.astype(jnp.bfloat16)
        mixed = (
            jnp.einsum("uqk,ukd->uqd", probs, value_flat, preferred_element_type=jnp.float32)
            / total
        )
        return mixed.astype(jnp.bfloat16)

    grouped = (
        slot_index.reshape(-1, group_size),
        tile_index.reshape(-1, group_size),
        head_index.reshape(-1, group_size),
    )
    result = lax.map(one_group, grouped)
    return result.reshape(-1, result.shape[2], result.shape[3])


def local_general(queries, keys, values, q_gain, k_gain, key_tiles, key_count):
    devices = lax.axis_size("seq")
    my_index = lax.axis_index("seq")
    q_normed = normed(queries, q_gain)
    k_normed = normed(keys, k_gain)
    stacked = (
        jnp.stack([q_normed, k_normed, values])
        .reshape(3, TILE, HEADS, HEAD_DIM)
        .transpose(2, 0, 1, 3)
    )
    targets = jnp.arange(devices)
    per_device = (HEADS + devices - 1) // devices
    total_slots = devices * per_device
    fewest_slots = total_slots // HEADS
    most_units = (devices + fewest_slots - 1) // fewest_slots

    def slot_layout(slot_number):
        head_of = slot_number * HEADS // total_slots
        head_start = (head_of * total_slots + HEADS - 1) // HEADS
        head_end = ((head_of + 1) * total_slots + HEADS - 1) // HEADS
        sharers = head_end - head_start
        within = slot_number - head_start
        return (head_of, within * devices // sharers, (within + 1) * devices // sharers)

    all_slots = jnp.arange(total_slots).reshape(devices, per_device)
    send_heads = slot_layout(all_slots)[0]
    received = lax.all_to_all(stacked[send_heads], "seq", split_axis=0, concat_axis=0, tiled=True)
    own_heads, lower_tile, upper_tile = slot_layout(my_index * per_device + jnp.arange(per_device))
    offsets = jnp.arange(most_units)
    tile_grid = jnp.minimum(lower_tile[:, None] + offsets[None, :], devices - 1)
    slot_grid = jnp.broadcast_to(jnp.arange(per_device)[:, None], tile_grid.shape)
    head_grid = jnp.broadcast_to(own_heads[:, None], tile_grid.shape)
    unit_total = per_device * most_units
    length = (unit_total + group_size - 1) // group_size * group_size
    finished = attend_units(
        received,
        padded(slot_grid.reshape(-1), length),
        padded(tile_grid.reshape(-1), length),
        padded(head_grid.reshape(-1), length),
        key_tiles,
        key_count,
    )[:unit_total]
    finished = finished.reshape(per_device, most_units, TILE, HEAD_DIM)
    position = targets[:, None] - lower_tile[None, :]
    inside = (position >= 0) & (targets[:, None] < upper_tile[None, :])
    gathered = finished[jnp.arange(per_device)[None, :], jnp.clip(position, 0, most_units - 1)]
    outgoing = jnp.where(inside[:, :, None, None], gathered, jnp.zeros_like(gathered))
    returned = lax.all_to_all(outgoing, "seq", split_axis=0, concat_axis=0, tiled=True)
    head_list = jnp.arange(HEADS)
    head_start = (head_list * total_slots + HEADS - 1) // HEADS
    sharers = ((head_list + 1) * total_slots + HEADS - 1) // HEADS - head_start
    owner_slot = head_start + ((my_index + 1) * sharers - 1) // devices
    pieces = returned[owner_slot // per_device, owner_slot % per_device]
    return pieces.transpose(1, 0, 2).reshape(TILE, HEADS * HEAD_DIM)


ALL_VMEM_BYTES = 60 * 1024 * 1024
IN_HBM = pl.BlockSpec(memory_space=pltpu.HBM)
ANYWHERE = pl.BlockSpec(memory_space=pl.ANY)
IN_SMEM = pl.BlockSpec(memory_space=pltpu.SMEM)
IN_VMEM = pl.BlockSpec(memory_space=pltpu.VMEM)
PARAMS = pltpu.CompilerParams(vmem_limit_bytes=ALL_VMEM_BYTES)
LEAVE_ROOM = pltpu.CompilerParams(vmem_limit_bytes=40 * 1024 * 1024)
LOADS = 2


def head_of(pair, core, slot, full):
    return pair * (2 * full + 1) + (full if slot == full else slot + core * (full + 1))


def columns_of(head):
    return slice(head * HEAD_DIM, (head + 1) * HEAD_DIM)


def traced_columns(head):
    return pl.ds(pl.multiple_of(head * HEAD_DIM, HEAD_DIM), HEAD_DIM)


def bf16(*shape):
    return jax.ShapeDtypeStruct(shape, jnp.bfloat16)


def copy_list(sems):
    return sems, []


def start_copy(copies, source, target):
    sems, started = copies
    started.append(pltpu.make_async_copy(source, target, sems.at[len(started)]))
    started[-1].start()
    return started[-1]


def wait_copies(copies):
    for copy in copies[1]:
        copy.wait()


def norm_in_place(rows, gain, loads, gain_load):
    count = TILE // len(loads)
    for part, load in enumerate(loads):
        here = slice(part * count, (part + 1) * count)
        load.wait()
        squares = jnp.zeros((count, HEAD_DIM), jnp.float32)
        for head in range(HEADS):
            block = rows[here, columns_of(head)].astype(jnp.float32)
            squares = squares + block * block
        mean = jnp.sum(squares, axis=-1, keepdims=True) / (HEADS * HEAD_DIM)
        factor = lax.rsqrt(mean + 1e-06)
        if part == 0:
            gain_load.wait()
        for head in range(HEADS):
            block = rows[here, columns_of(head)].astype(jnp.float32)
            scaled = block * factor * gain[columns_of(head)][None, :]
            rows[here, columns_of(head)] = scaled.astype(jnp.bfloat16)


def prepare_kernel(send, queries, keys, values, q_gain, k_gain, scratch):
    q_rows, k_rows, v_rows, q_scale, k_scale, in_sems = scratch
    loading = copy_list(in_sems)

    def load(source, target):
        parts = [pl.ds(i * TILE // LOADS, TILE // LOADS) for i in range(LOADS)]
        return [start_copy(loading, source.at[part], target.at[part]) for part in parts]

    k_scale_load = start_copy(loading, k_gain, k_scale)
    q_scale_load = start_copy(loading, q_gain, q_scale)
    k_loads, v_loads, q_loads = load(keys, k_rows), load(values, v_rows), load(queries, q_rows)
    norm_in_place(k_rows, k_scale, k_loads, k_scale_load)
    send(k_rows, 1)
    for part in v_loads:
        part.wait()
    send(v_rows, 2)
    norm_in_place(q_rows, q_scale, q_loads, q_scale_load)
    send(q_rows, 0)


def prepare_whole_kernel(full, *refs):
    operands, out, scratch, out_sems = refs[:5], refs[5], refs[6:-1], refs[-1]
    copies = copy_list(out_sems)

    def send(rows, tensor):
        for device in range(out.shape[0]):
            for slot in range(full):
                head = head_of(device // 2, device % 2, slot, full)
                target = out.at[device, pl.ds((3 * slot + tensor) * TILE, TILE)]
                start_copy(copies, rows.at[:, pl.ds(head * HEAD_DIM, HEAD_DIM)], target)

    prepare_kernel(send, *operands, scratch)
    wait_copies(copies)


def prepare_shared_kernel(full, me_ref, *refs):
    operands, outs, scratch, out_sems = refs[:5], refs[5:7], refs[7:-1], refs[-1]
    copies = copy_list(out_sems)

    def send(rows, tensor):
        for odd, out in enumerate(outs):
            for flip in range(out.shape[0]):
                pair = jnp.bitwise_xor(me_ref[0] // 2, 2 * flip + odd)
                target = out.at[flip, pl.ds(tensor * TILE, TILE)]
                source = rows.at[:, traced_columns(head_of(pair, 0, full, full))]
                start_copy(copies, source, target)

    prepare_kernel(send, *operands, scratch)
    wait_copies(copies)


def prepare_scratch(queries, q_gain, copies):
    rows = pltpu.VMEM(queries.shape, jnp.bfloat16)
    scale = pltpu.VMEM(q_gain.shape, jnp.float32)
    sems = pltpu.SemaphoreType.DMA
    return [rows, rows, rows, scale, scale, sems((3 * LOADS + 2,)), sems((copies,))]


def prepare_whole(full, devices, *operands):
    return pl.pallas_call(
        functools.partial(prepare_whole_kernel, full),
        name="prepare_whole",
        out_shape=bf16(devices, 3 * full * TILE, HEAD_DIM),
        in_specs=[IN_HBM] * 5,
        out_specs=ANYWHERE,
        scratch_shapes=prepare_scratch(operands[0], operands[3], 3 * full * devices),
        compiler_params=PARAMS,
    )(*operands)


def prepare_shared(full, pairs, me, *operands):
    return pl.pallas_call(
        functools.partial(prepare_shared_kernel, full),
        name="prepare_shared",
        out_shape=[bf16(pairs // 2, 3 * TILE, HEAD_DIM)] * 2,
        in_specs=[IN_SMEM] + [IN_HBM] * 5,
        out_specs=[ANYWHERE] * 2,
        scratch_shapes=prepare_scratch(operands[0], operands[3], 3 * pairs),
        compiler_params=PARAMS,
    )(me, *operands)


def join_columns_kernel(own, other, *refs):
    outs, (rows, in_sems, out_sems) = refs[:-3], refs[-3:]
    count = own.shape[1]
    loads, stores = copy_list(in_sems), copy_list(out_sems)
    for flip in range(len(outs)):
        start_copy(loads, own.at[flip], rows.at[flip, pl.ds(0, count)])
        start_copy(loads, other.at[flip], rows.at[flip, pl.ds(count, count)])
    for flip, out in enumerate(outs):
        loads[1][2 * flip].wait()
        loads[1][2 * flip + 1].wait()
        start_copy(stores, rows.at[flip], out)
    wait_copies(stores)


def join_columns(own, other):
    flips, count = own.shape[:2]
    return pl.pallas_call(
        join_columns_kernel,
        name="join_columns",
        out_shape=[bf16(2 * count, HEAD_DIM)] * flips,
        in_specs=[ANYWHERE] * 2,
        out_specs=[ANYWHERE] * flips,
        scratch_shapes=[
            pltpu.VMEM((flips, 2 * count, HEAD_DIM), jnp.bfloat16),
            pltpu.SemaphoreType.DMA((2 * flips,)),
            pltpu.SemaphoreType.DMA((flips,)),
        ],
        compiler_params=LEAVE_ROOM,
    )(own, other)


UNROLL = 4


def write_marks(marked):
    shape = (marked.shape[0], HEAD_DIM)
    tile = lax.broadcasted_iota(jnp.int32, shape, 0) // TILE
    marks = jnp.where(lax.broadcasted_iota(jnp.int32, shape, 1) == tile, 1.0, 0.0)
    marked[:, HEAD_DIM:] = marks.astype(jnp.bfloat16)


def query_masks(queries, mask):
    bit = jnp.minimum(lax.broadcasted_iota(jnp.int32, (1, HEAD_DIM), 1), 31)
    offsets = jnp.where((mask >> bit) & 1 == 1, jnp.float32(0.0), jnp.float32(-1e30))
    offsets = jnp.broadcast_to(offsets, queries.shape).astype(jnp.bfloat16)
    return jnp.concatenate([queries, offsets], axis=1)


def attend_rows(queries, keys, values, masks):
    tiles = keys.shape[0] // TILE
    marked = [query_masks(tile, mask) for tile, mask in zip(queries, masks)]
    scores = lax.dot_general(
        jnp.concatenate(marked, axis=0),
        keys,
        (((1,), (1,)), ((), ())),
        preferred_element_type=jnp.float32,
    )
    scale = jnp.float32(math.log2(math.e) / math.sqrt(HEAD_DIM))
    probs, totals = [], []
    for i in range(len(masks)):
        rows = slice(i * TILE, (i + 1) * TILE)
        parts = [scores[rows, tile * TILE : (tile + 1) * TILE] for tile in range(tiles)]
        peak = jnp.max(functools.reduce(jnp.maximum, parts), axis=-1, keepdims=True)
        weights = [jnp.exp2((part - peak) * scale) for part in parts]
        totals.append(jnp.sum(functools.reduce(jnp.add, weights), axis=-1, keepdims=True))
        probs.append(jnp.concatenate([w.astype(jnp.bfloat16) for w in weights], axis=1))
    mixed = jnp.dot(jnp.concatenate(probs, axis=0), values, preferred_element_type=jnp.float32)
    return [
        (mixed[i * TILE : (i + 1) * TILE] / total).astype(jnp.bfloat16)
        for i, total in enumerate(totals)
    ]


def attend_slot(mask_ref, slot, here, first, out, out_first, stride, together, marked):
    def part(tile, tensor):
        return here[tile, first + tensor * TILE : first + (tensor + 1) * TILE]

    marked[:, :HEAD_DIM] = part(slice(None), 1).reshape(-1, HEAD_DIM)

    products = here.shape[0] // (stride * together)
    unroll = math.gcd(products, UNROLL)

    def step(index, carry):
        for product in range(unroll):
            at = (index * unroll + product) * together
            tiles = [(at + i) * stride for i in range(together)]
            values = part(slice(None), 2).reshape(-1, HEAD_DIM)
            masks = [mask_ref[slot, tile] for tile in tiles]
            blocks = attend_rows([part(tile, 0) for tile in tiles], marked[...], values, masks)
            for tile, block in zip(tiles, blocks):
                out[tile, out_first : out_first + TILE] = block
        return carry

    lax.fori_loop(0, products // unroll, step, 0)


def marked_keys(devices):
    return pltpu.VMEM((devices * TILE, 2 * HEAD_DIM), jnp.bfloat16)


def attend_whole_kernel(full, mask_ref, here, outs, out, marked, sems):
    stores = copy_list(sems)
    write_marks(marked)
    for slot in range(full):
        attend_slot(mask_ref, slot, here, 3 * slot * TILE, out, slot * TILE, 1, 4, marked)
        rows = pl.ds(slot * TILE, TILE)
        start_copy(stores, out.at[:, rows], outs.at[:, rows])
    wait_copies(stores)


def attend_whole(full, masks, here):
    shape = (here.shape[0], full * TILE, HEAD_DIM)
    return pl.pallas_call(
        functools.partial(attend_whole_kernel, full),
        name="attend_whole",
        out_shape=bf16(*shape),
        in_specs=[IN_SMEM, IN_VMEM],
        out_specs=IN_HBM,
        scratch_shapes=[
            pltpu.VMEM(shape, jnp.bfloat16),
            marked_keys(here.shape[0]),
            pltpu.SemaphoreType.DMA((full,)),
        ],
        compiler_params=PARAMS,
    )(masks, here)


def attend_shared_kernel(full, mask_ref, *refs):
    blocks, (other, *outs), scratch = refs[:-8], refs[-8:-5], refs[-5:]
    here, out, marked, in_sems, out_sems = scratch
    loads, stores = copy_list(in_sems), copy_list(out_sems)
    for flip, block in enumerate(blocks):
        for odd in range(2):
            partner = 2 * flip + odd
            start_copy(loads, block.at[pl.ds(3 * odd * TILE, 3 * TILE)], here.at[2 * partner])
            target = here.at[2 * partner + 1, pl.ds(TILE, 2 * TILE)]
            start_copy(loads, other.at[partner], target)
    write_marks(marked)
    wait_copies(loads)
    attend_slot(mask_ref, full, here, 0, out, 0, 2, 2, marked)
    for flip in range(len(blocks)):
        for odd in range(2):
            start_copy(stores, out.at[2 * (2 * flip + odd)], outs[odd].at[flip])
    wait_copies(stores)


def attend_shared(full, masks, blocks, other):
    flips = len(blocks)
    return pl.pallas_call(
        functools.partial(attend_shared_kernel, full),
        name="attend_shared",
        out_shape=[bf16(flips, TILE, HEAD_DIM)] * 2,
        in_specs=[IN_SMEM] + [ANYWHERE] * (flips + 1),
        out_specs=[ANYWHERE] * 2,
        scratch_shapes=[
            pltpu.VMEM((4 * flips, 3 * TILE, HEAD_DIM), jnp.bfloat16),
            pltpu.VMEM((4 * flips, TILE, HEAD_DIM), jnp.bfloat16),
            marked_keys(4 * flips),
            pltpu.SemaphoreType.DMA((4 * flips,)),
            pltpu.SemaphoreType.DMA((2 * flips,)),
        ],
        compiler_params=LEAVE_ROOM,
    )(masks, *blocks, other)


def join_keys_values_kernel(*refs):
    blocks, (out, rows, in_sems, out_sems) = refs[:-4], refs[-4:]
    loads, stores = copy_list(in_sems), copy_list(out_sems)
    for partner in range(2 * len(blocks)):
        source = blocks[partner // 2].at[pl.ds((3 * (partner % 2) + 1) * TILE, 2 * TILE)]
        start_copy(loads, source, rows.at[partner])
    for partner, load in enumerate(loads[1]):
        load.wait()
        start_copy(stores, rows.at[partner], out.at[partner])
    wait_copies(stores)


def join_keys_values(blocks):
    shape = (2 * len(blocks), 2 * TILE, HEAD_DIM)
    sems = pltpu.SemaphoreType.DMA((2 * len(blocks),))
    return pl.pallas_call(
        join_keys_values_kernel,
        name="join_keys_values",
        out_shape=bf16(*shape),
        in_specs=[ANYWHERE] * len(blocks),
        out_specs=ANYWHERE,
        scratch_shapes=[pltpu.VMEM(shape, jnp.bfloat16), sems, sems],
        compiler_params=LEAVE_ROOM,
    )(*blocks)


def collect_shared_kernel(full, me_ref, *refs):
    blocks, (_, out, rows, in_sems, out_sems) = refs[:-5], refs[-5:]
    loads, stores = copy_list(in_sems), copy_list(out_sems)
    for flip, block in enumerate(blocks):
        start_copy(loads, block, rows.at[flip])
    for flip, load in enumerate(loads[1]):
        load.wait()
        for odd in range(2):
            pair = jnp.bitwise_xor(me_ref[0] // 2, 2 * flip + odd)
            target = out.at[:, traced_columns(head_of(pair, 0, full, full))]
            start_copy(stores, rows.at[flip, pl.ds(odd * TILE, TILE)], target)
    wait_copies(stores)


def collect_shared(full, me, blocks, so_far):
    flips = len(blocks)
    return pl.pallas_call(
        functools.partial(collect_shared_kernel, full),
        name="collect_shared",
        out_shape=bf16(*so_far.shape),
        in_specs=[IN_SMEM] + [ANYWHERE] * flips + [IN_HBM],
        out_specs=IN_HBM,
        scratch_shapes=[
            pltpu.VMEM((flips, 2 * TILE, HEAD_DIM), jnp.bfloat16),
            pltpu.SemaphoreType.DMA((flips,)),
            pltpu.SemaphoreType.DMA((2 * flips,)),
        ],
        input_output_aliases={1 + flips: 0},
        compiler_params=LEAVE_ROOM,
    )(me, *blocks, so_far)


def collect_whole_kernel(full, here, out, sems):
    stores = copy_list(sems)
    for device in range(here.shape[0]):
        for slot in range(full):
            head = head_of(device // 2, device % 2, slot, full)
            target = out.at[:, pl.ds(head * HEAD_DIM, HEAD_DIM)]
            start_copy(stores, here.at[device, pl.ds(slot * TILE, TILE)], target)
    wait_copies(stores)


def collect_whole(full, shape, here):
    return pl.pallas_call(
        functools.partial(collect_whole_kernel, full),
        name="collect_whole",
        out_shape=bf16(*shape),
        in_specs=[IN_VMEM],
        out_specs=IN_HBM,
        scratch_shapes=[pltpu.SemaphoreType.DMA((full * here.shape[0],))],
        compiler_params=LEAVE_ROOM,
    )(here)


def with_all(blocks):
    return lax.all_to_all(blocks, "seq", split_axis=0, concat_axis=0, tiled=True)


def with_partner(block, k):
    devices = lax.axis_size("seq")
    return lax.ppermute(block, "seq", [(i, i ^ (2 * k)) for i in range(devices)]) if k else block


def with_sibling(block):
    return lax.ppermute(block, "seq", [(i, i ^ 1) for i in range(lax.axis_size("seq"))])


def after(value, *others):
    return lax.optimization_barrier((value, *others))[0]


def all_after(values, *others):
    return list(lax.optimization_barrier((*values, *others))[: len(values)])


def tile_masks(full, my_index, key_tiles, key_count):
    slots = jnp.arange(full + 1)
    within = jnp.where(slots < full, slots + my_index % 2 * (full + 1), full)
    heads = my_index // 2 * (2 * full + 1) + within
    tiles, counts = key_tiles[heads], key_count[heads]
    flip = jnp.where(slots < full, 0, my_index)
    bits = jnp.left_shift(1, jnp.bitwise_xor(tiles, flip[:, None, None]))
    allowed = jnp.arange(tiles.shape[-1]) < counts[:, :, None]
    masks = jnp.sum(jnp.where(allowed, bits, 0), axis=-1)
    order = jnp.bitwise_xor(jnp.arange(tiles.shape[1])[None, :], flip[:, None])
    return jnp.take_along_axis(masks, order, axis=1)


def local_paired(queries, keys, values, q_gain, k_gain, key_tiles, key_count):
    devices = lax.axis_size("seq")
    pairs = devices // 2
    full = HEADS // devices
    my_index = lax.axis_index("seq")
    me = my_index.reshape(1)
    rest = (keys, values, q_gain, k_gain)

    whole = prepare_whole(full, devices, queries, *rest)
    masks = tile_masks(full, my_index, key_tiles, key_count)
    even, odd = prepare_shared(full, pairs, me, after(queries, masks, whole), *rest)
    whole = with_all(whole)
    shared = join_columns(even, with_partner(odd, 1))
    near, far = shared[: pairs // 4], shared[pairs // 4 :]
    near = [with_partner(block, 2 * flip) for flip, block in enumerate(near)]
    whole = after(whole, *near, *far)
    far = all_after(far, whole)
    far = [with_partner(block, 2 * flip + pairs // 2) for flip, block in enumerate(far)]
    whole_out = attend_whole(full, masks, whole)
    shared = all_after(near + far, whole_out)
    whole_back = with_all(after(whole_out, *shared))
    other = with_sibling(join_keys_values(shared))
    even, odd = attend_shared(full, masks, shared, other)
    shared_back = join_columns(even, with_partner(odd, 1))
    shared_back = [with_partner(block, 2 * flip) for flip, block in enumerate(shared_back)]
    so_far = collect_whole(full, queries.shape, whole_back)
    return collect_shared(full, me, shared_back, so_far)


def paired_fits(mesh, key_tiles_shape):
    devices = mesh.shape["seq"]
    per_pair, rest = divmod(2 * HEADS, devices)
    return (
        rest == 0
        and per_pair % 2 == 1
        and per_pair >= 3
        and devices >= 16
        and devices & (devices - 1) == 0
        and key_tiles_shape[1] == devices
        and devices <= 31
    )


def solution(mesh):
    in_specs = (
        P(("groups", "seq"), None),
        P(("groups", "seq"), None),
        P(("groups", "seq"), None),
        P(),
        P(),
        P(),
        P(),
    )
    out_specs = P(("groups", "seq"), None)

    def run(*operands):
        paired = paired_fits(mesh, operands[5].shape)
        body = local_paired if paired else local_general
        return jax.shard_map(
            body, mesh=mesh, in_specs=in_specs, out_specs=out_specs, check_vma=False
        )(*operands)

    return run
```

```python
import functools
import math

import jax
import jax.numpy as jnp
from jax import lax
from jax.experimental import pallas as pl
from jax.experimental.pallas import tpu as pltpu
from jax.sharding import PartitionSpec as P

HEADS = 40
HEAD_DIM = 128
TILE = 128


group_size = 4


def normed(rows, gain):
    values32 = rows.astype(jnp.float32)
    factor = lax.rsqrt(jnp.mean(values32 * values32, axis=-1, keepdims=True) + 1e-06)
    return (values32 * factor * gain).astype(jnp.bfloat16)


def padded(entries, length):
    return jnp.pad(entries, (0, length - entries.shape[0]), mode="edge")


def attend_units(received, slot_index, tile_index, head_index, key_tiles, key_count):

    def one_group(unit_items):
        slot_part, tile_part, head_part = unit_items
        query_rows = received[tile_part, slot_part, 0]
        key_lists = key_tiles[head_part, tile_part]
        counts = key_count[head_part, tile_part]
        key_block = received[key_lists, slot_part[:, None], 1]
        value_block = received[key_lists, slot_part[:, None], 2]
        units = query_rows.shape[0]
        tile_rows = query_rows.shape[1]
        key_flat = key_block.reshape(units, -1, key_block.shape[-1])
        value_flat = value_block.reshape(units, -1, value_block.shape[-1])
        scores = jnp.einsum(
            "uqd,ukd->uqk", query_rows, key_flat, preferred_element_type=jnp.float32
        ) / math.sqrt(query_rows.shape[-1])
        list_place = jnp.arange(key_flat.shape[1]) // tile_rows
        valid = (list_place[None, :] < counts[:, None])[:, None, :]
        masked = jnp.where(valid, scores, -jnp.inf)
        peak = jnp.max(masked, axis=-1, keepdims=True)
        weights = jnp.where(valid, jnp.exp(masked - peak), jnp.float32(0.0))
        total = jnp.sum(weights, axis=-1, keepdims=True)
        probs = weights.astype(jnp.bfloat16)
        mixed = (
            jnp.einsum("uqk,ukd->uqd", probs, value_flat, preferred_element_type=jnp.float32)
            / total
        )
        return mixed.astype(jnp.bfloat16)

    grouped = (
        slot_index.reshape(-1, group_size),
        tile_index.reshape(-1, group_size),
        head_index.reshape(-1, group_size),
    )
    result = lax.map(one_group, grouped)
    return result.reshape(-1, result.shape[2], result.shape[3])


def local_general(queries, keys, values, q_gain, k_gain, key_tiles, key_count):
    devices = lax.axis_size("seq")
    my_index = lax.axis_index("seq")
    q_normed = normed(queries, q_gain)
    k_normed = normed(keys, k_gain)
    stacked = (
        jnp.stack([q_normed, k_normed, values])
        .reshape(3, TILE, HEADS, HEAD_DIM)
        .transpose(2, 0, 1, 3)
    )
    targets = jnp.arange(devices)
    per_device = (HEADS + devices - 1) // devices
    total_slots = devices * per_device
    fewest_slots = total_slots // HEADS
    most_units = (devices + fewest_slots - 1) // fewest_slots

    def slot_layout(slot_number):
        head_of = slot_number * HEADS // total_slots
        head_start = (head_of * total_slots + HEADS - 1) // HEADS
        head_end = ((head_of + 1) * total_slots + HEADS - 1) // HEADS
        sharers = head_end - head_start
        within = slot_number - head_start
        return (head_of, within * devices // sharers, (within + 1) * devices // sharers)

    all_slots = jnp.arange(total_slots).reshape(devices, per_device)
    send_heads = slot_layout(all_slots)[0]
    received = lax.all_to_all(stacked[send_heads], "seq", split_axis=0, concat_axis=0, tiled=True)
    own_heads, lower_tile, upper_tile = slot_layout(my_index * per_device + jnp.arange(per_device))
    offsets = jnp.arange(most_units)
    tile_grid = jnp.minimum(lower_tile[:, None] + offsets[None, :], devices - 1)
    slot_grid = jnp.broadcast_to(jnp.arange(per_device)[:, None], tile_grid.shape)
    head_grid = jnp.broadcast_to(own_heads[:, None], tile_grid.shape)
    unit_total = per_device * most_units
    length = (unit_total + group_size - 1) // group_size * group_size
    finished = attend_units(
        received,
        padded(slot_grid.reshape(-1), length),
        padded(tile_grid.reshape(-1), length),
        padded(head_grid.reshape(-1), length),
        key_tiles,
        key_count,
    )[:unit_total]
    finished = finished.reshape(per_device, most_units, TILE, HEAD_DIM)
    position = targets[:, None] - lower_tile[None, :]
    inside = (position >= 0) & (targets[:, None] < upper_tile[None, :])
    gathered = finished[jnp.arange(per_device)[None, :], jnp.clip(position, 0, most_units - 1)]
    outgoing = jnp.where(inside[:, :, None, None], gathered, jnp.zeros_like(gathered))
    returned = lax.all_to_all(outgoing, "seq", split_axis=0, concat_axis=0, tiled=True)
    head_list = jnp.arange(HEADS)
    head_start = (head_list * total_slots + HEADS - 1) // HEADS
    sharers = ((head_list + 1) * total_slots + HEADS - 1) // HEADS - head_start
    owner_slot = head_start + ((my_index + 1) * sharers - 1) // devices
    pieces = returned[owner_slot // per_device, owner_slot % per_device]
    return pieces.transpose(1, 0, 2).reshape(TILE, HEADS * HEAD_DIM)


ALL_VMEM_BYTES = 60 * 1024 * 1024
IN_HBM = pl.BlockSpec(memory_space=pltpu.HBM)
ANYWHERE = pl.BlockSpec(memory_space=pl.ANY)
IN_SMEM = pl.BlockSpec(memory_space=pltpu.SMEM)
IN_VMEM = pl.BlockSpec(memory_space=pltpu.VMEM)
PARAMS = pltpu.CompilerParams(vmem_limit_bytes=ALL_VMEM_BYTES)
LEAVE_ROOM = pltpu.CompilerParams(vmem_limit_bytes=40 * 1024 * 1024)
LOADS = 2


def head_of(pair, core, slot, full):
    return pair * (2 * full + 1) + (full if slot == full else slot + core * (full + 1))


def columns_of(head):
    return slice(head * HEAD_DIM, (head + 1) * HEAD_DIM)


def traced_columns(head):
    return pl.ds(pl.multiple_of(head * HEAD_DIM, HEAD_DIM), HEAD_DIM)


def bf16(*shape):
    return jax.ShapeDtypeStruct(shape, jnp.bfloat16)


def copy_list(sems):
    return sems, []


def start_copy(copies, source, target):
    sems, started = copies
    started.append(pltpu.make_async_copy(source, target, sems.at[len(started)]))
    started[-1].start()
    return started[-1]


def wait_copies(copies):
    for copy in copies[1]:
        copy.wait()


def norm_in_place(rows, gain, loads, gain_load):
    count = TILE // len(loads)
    for part, load in enumerate(loads):
        here = slice(part * count, (part + 1) * count)
        load.wait()
        squares = jnp.zeros((count, HEAD_DIM), jnp.float32)
        for head in range(HEADS):
            block = rows[here, columns_of(head)].astype(jnp.float32)
            squares = squares + block * block
        mean = jnp.sum(squares, axis=-1, keepdims=True) / (HEADS * HEAD_DIM)
        factor = lax.rsqrt(mean + 1e-06)
        if part == 0:
            gain_load.wait()
        for head in range(HEADS):
            block = rows[here, columns_of(head)].astype(jnp.float32)
            scaled = block * factor * gain[columns_of(head)][None, :]
            rows[here, columns_of(head)] = scaled.astype(jnp.bfloat16)


def prepare_kernel(send, queries, keys, values, q_gain, k_gain, scratch):
    q_rows, k_rows, v_rows, q_scale, k_scale, in_sems = scratch
    loading = copy_list(in_sems)

    def load(source, target):
        parts = [pl.ds(i * TILE // LOADS, TILE // LOADS) for i in range(LOADS)]
        return [start_copy(loading, source.at[part], target.at[part]) for part in parts]

    k_scale_load = start_copy(loading, k_gain, k_scale)
    q_scale_load = start_copy(loading, q_gain, q_scale)
    k_loads, v_loads, q_loads = load(keys, k_rows), load(values, v_rows), load(queries, q_rows)
    norm_in_place(k_rows, k_scale, k_loads, k_scale_load)
    send(k_rows, 1)
    for part in v_loads:
        part.wait()
    send(v_rows, 2)
    norm_in_place(q_rows, q_scale, q_loads, q_scale_load)
    send(q_rows, 0)


def prepare_whole_kernel(full, *refs):
    operands, out, scratch, out_sems = refs[:5], refs[5], refs[6:-1], refs[-1]
    copies = copy_list(out_sems)

    def send(rows, tensor):
        for device in range(out.shape[0]):
            for slot in range(full):
                head = head_of(device // 2, device % 2, slot, full)
                target = out.at[device, pl.ds((3 * slot + tensor) * TILE, TILE)]
                start_copy(copies, rows.at[:, pl.ds(head * HEAD_DIM, HEAD_DIM)], target)

    prepare_kernel(send, *operands, scratch)
    wait_copies(copies)


def prepare_shared_kernel(full, me_ref, *refs):
    operands, outs, scratch, out_sems = refs[:5], refs[5:7], refs[7:-1], refs[-1]
    copies = copy_list(out_sems)

    def send(rows, tensor):
        for odd, out in enumerate(outs):
            for flip in range(out.shape[0]):
                pair = jnp.bitwise_xor(me_ref[0] // 2, 2 * flip + odd)
                target = out.at[flip, pl.ds(tensor * TILE, TILE)]
                source = rows.at[:, traced_columns(head_of(pair, 0, full, full))]
                start_copy(copies, source, target)

    prepare_kernel(send, *operands, scratch)
    wait_copies(copies)


def prepare_scratch(queries, q_gain, copies):
    rows = pltpu.VMEM(queries.shape, jnp.bfloat16)
    scale = pltpu.VMEM(q_gain.shape, jnp.float32)
    sems = pltpu.SemaphoreType.DMA
    return [rows, rows, rows, scale, scale, sems((3 * LOADS + 2,)), sems((copies,))]


def prepare_whole(full, devices, *operands):
    return pl.pallas_call(
        functools.partial(prepare_whole_kernel, full),
        name="prepare_whole",
        out_shape=bf16(devices, 3 * full * TILE, HEAD_DIM),
        in_specs=[IN_HBM] * 5,
        out_specs=ANYWHERE,
        scratch_shapes=prepare_scratch(operands[0], operands[3], 3 * full * devices),
        compiler_params=PARAMS,
    )(*operands)


def prepare_shared(full, pairs, me, *operands):
    return pl.pallas_call(
        functools.partial(prepare_shared_kernel, full),
        name="prepare_shared",
        out_shape=[bf16(pairs // 2, 3 * TILE, HEAD_DIM)] * 2,
        in_specs=[IN_SMEM] + [IN_HBM] * 5,
        out_specs=[ANYWHERE] * 2,
        scratch_shapes=prepare_scratch(operands[0], operands[3], 3 * pairs),
        compiler_params=PARAMS,
    )(me, *operands)


def join_columns_kernel(own, other, *refs):
    outs, (rows, in_sems, out_sems) = refs[:-3], refs[-3:]
    count = own.shape[1]
    loads, stores = copy_list(in_sems), copy_list(out_sems)
    for flip in range(len(outs)):
        start_copy(loads, own.at[flip], rows.at[flip, pl.ds(0, count)])
        start_copy(loads, other.at[flip], rows.at[flip, pl.ds(count, count)])
    for flip, out in enumerate(outs):
        loads[1][2 * flip].wait()
        loads[1][2 * flip + 1].wait()
        start_copy(stores, rows.at[flip], out)
    wait_copies(stores)


def join_columns(own, other):
    flips, count = own.shape[:2]
    return pl.pallas_call(
        join_columns_kernel,
        name="join_columns",
        out_shape=[bf16(2 * count, HEAD_DIM)] * flips,
        in_specs=[ANYWHERE] * 2,
        out_specs=[ANYWHERE] * flips,
        scratch_shapes=[
            pltpu.VMEM((flips, 2 * count, HEAD_DIM), jnp.bfloat16),
            pltpu.SemaphoreType.DMA((2 * flips,)),
            pltpu.SemaphoreType.DMA((flips,)),
        ],
        compiler_params=LEAVE_ROOM,
    )(own, other)


UNROLL = 4


def write_marks(marked):
    shape = (marked.shape[0], HEAD_DIM)
    tile = lax.broadcasted_iota(jnp.int32, shape, 0) // TILE
    marks = jnp.where(lax.broadcasted_iota(jnp.int32, shape, 1) == tile, 1.0, 0.0)
    marked[:, HEAD_DIM:] = marks.astype(jnp.bfloat16)


def query_masks(queries, mask):
    bit = jnp.minimum(lax.broadcasted_iota(jnp.int32, (1, HEAD_DIM), 1), 31)
    offsets = jnp.where((mask >> bit) & 1 == 1, jnp.float32(0.0), jnp.float32(-1e30))
    offsets = jnp.broadcast_to(offsets, queries.shape).astype(jnp.bfloat16)
    return jnp.concatenate([queries, offsets], axis=1)


def attend_rows(queries, keys, values, masks):
    tiles = keys.shape[0] // TILE
    marked = [query_masks(tile, mask) for tile, mask in zip(queries, masks)]
    scores = lax.dot_general(
        jnp.concatenate(marked, axis=0),
        keys,
        (((1,), (1,)), ((), ())),
        preferred_element_type=jnp.float32,
    )
    scale = jnp.float32(math.log2(math.e) / math.sqrt(HEAD_DIM))
    probs, totals = [], []
    for i in range(len(masks)):
        rows = slice(i * TILE, (i + 1) * TILE)
        parts = [scores[rows, tile * TILE : (tile + 1) * TILE] for tile in range(tiles)]
        peak = jnp.max(functools.reduce(jnp.maximum, parts), axis=-1, keepdims=True)
        weights = [jnp.exp2((part - peak) * scale) for part in parts]
        totals.append(jnp.sum(functools.reduce(jnp.add, weights), axis=-1, keepdims=True))
        probs.append(jnp.concatenate([w.astype(jnp.bfloat16) for w in weights], axis=1))
    mixed = jnp.dot(jnp.concatenate(probs, axis=0), values, preferred_element_type=jnp.float32)
    return [
        (mixed[i * TILE : (i + 1) * TILE] / total).astype(jnp.bfloat16)
        for i, total in enumerate(totals)
    ]


def attend_slot(mask_ref, slot, here, first, out, out_first, stride, together, marked, stored):
    def part(tile, tensor):
        return here[tile, first + tensor * TILE : first + (tensor + 1) * TILE]

    marked[:, :HEAD_DIM] = part(slice(None), 1).reshape(-1, HEAD_DIM)

    products = here.shape[0] // (stride * together)
    unroll = math.gcd(products, UNROLL)

    def step(index, carry):
        for product in range(unroll):
            at = (index * unroll + product) * together
            tiles = [(at + i) * stride for i in range(together)]
            values = part(slice(None), 2).reshape(-1, HEAD_DIM)
            masks = [mask_ref[slot, tile] for tile in tiles]
            blocks = attend_rows([part(tile, 0) for tile in tiles], marked[...], values, masks)
            for tile, block in zip(tiles, blocks):
                out[tile, out_first : out_first + TILE] = block
            stored(at)
        return carry

    for index in range(products // unroll):
        step(index, 0)


def marked_keys(devices):
    return pltpu.VMEM((devices * TILE, 2 * HEAD_DIM), jnp.bfloat16)


def attend_whole_kernel(full, mask_ref, here, outs, out, marked, sems):
    stores = copy_list(sems)
    write_marks(marked)
    for slot in range(full):
        rows = pl.ds(slot * TILE, TILE)

        def stored(tile, rows=rows):
            tiles = pl.ds(tile, 4)
            start_copy(stores, out.at[tiles, rows], outs.at[tiles, rows])

        attend_slot(mask_ref, slot, here, 3 * slot * TILE, out, slot * TILE, 1, 4, marked, stored)
    wait_copies(stores)


def attend_whole(full, masks, here):
    shape = (here.shape[0], full * TILE, HEAD_DIM)
    return pl.pallas_call(
        functools.partial(attend_whole_kernel, full),
        name="attend_whole",
        out_shape=bf16(*shape),
        in_specs=[IN_SMEM, IN_VMEM],
        out_specs=IN_HBM,
        scratch_shapes=[
            pltpu.VMEM(shape, jnp.bfloat16),
            marked_keys(here.shape[0]),
            pltpu.SemaphoreType.DMA((full * here.shape[0] // 4,)),
        ],
        compiler_params=PARAMS,
    )(masks, here)


def attend_shared_kernel(full, mask_ref, *refs):
    blocks, (other, *outs), scratch = refs[:-8], refs[-8:-5], refs[-5:]
    here, out, marked, in_sems, out_sems = scratch
    loads, stores = copy_list(in_sems), copy_list(out_sems)
    for flip, block in enumerate(blocks):
        for odd in range(2):
            partner = 2 * flip + odd
            start_copy(loads, block.at[pl.ds(3 * odd * TILE, 3 * TILE)], here.at[2 * partner])
            target = here.at[2 * partner + 1, pl.ds(TILE, 2 * TILE)]
            start_copy(loads, other.at[partner], target)
    write_marks(marked)
    wait_copies(loads)
    attend_slot(mask_ref, full, here, 0, out, 0, 2, 2, marked, lambda tile: None)
    for flip in range(len(blocks)):
        for odd in range(2):
            start_copy(stores, out.at[2 * (2 * flip + odd)], outs[odd].at[flip])
    wait_copies(stores)


def attend_shared(full, masks, blocks, other):
    flips = len(blocks)
    return pl.pallas_call(
        functools.partial(attend_shared_kernel, full),
        name="attend_shared",
        out_shape=[bf16(flips, TILE, HEAD_DIM)] * 2,
        in_specs=[IN_SMEM] + [ANYWHERE] * (flips + 1),
        out_specs=[ANYWHERE] * 2,
        scratch_shapes=[
            pltpu.VMEM((4 * flips, 3 * TILE, HEAD_DIM), jnp.bfloat16),
            pltpu.VMEM((4 * flips, TILE, HEAD_DIM), jnp.bfloat16),
            marked_keys(4 * flips),
            pltpu.SemaphoreType.DMA((4 * flips,)),
            pltpu.SemaphoreType.DMA((2 * flips,)),
        ],
        compiler_params=LEAVE_ROOM,
    )(masks, *blocks, other)


def join_keys_values_kernel(*refs):
    blocks, (out, rows, in_sems, out_sems) = refs[:-4], refs[-4:]
    loads, stores = copy_list(in_sems), copy_list(out_sems)
    for partner in range(2 * len(blocks)):
        source = blocks[partner // 2].at[pl.ds((3 * (partner % 2) + 1) * TILE, 2 * TILE)]
        start_copy(loads, source, rows.at[partner])
    for partner, load in enumerate(loads[1]):
        load.wait()
        start_copy(stores, rows.at[partner], out.at[partner])
    wait_copies(stores)


def join_keys_values(blocks):
    shape = (2 * len(blocks), 2 * TILE, HEAD_DIM)
    sems = pltpu.SemaphoreType.DMA((2 * len(blocks),))
    return pl.pallas_call(
        join_keys_values_kernel,
        name="join_keys_values",
        out_shape=bf16(*shape),
        in_specs=[ANYWHERE] * len(blocks),
        out_specs=ANYWHERE,
        scratch_shapes=[pltpu.VMEM(shape, jnp.bfloat16), sems, sems],
        compiler_params=LEAVE_ROOM,
    )(*blocks)


def collect_shared_kernel(full, me_ref, *refs):
    blocks, (_, out, rows, in_sems, out_sems) = refs[:-5], refs[-5:]
    loads, stores = copy_list(in_sems), copy_list(out_sems)
    for flip, block in enumerate(blocks):
        start_copy(loads, block, rows.at[flip])
    for flip, load in enumerate(loads[1]):
        load.wait()
        for odd in range(2):
            pair = jnp.bitwise_xor(me_ref[0] // 2, 2 * flip + odd)
            target = out.at[:, traced_columns(head_of(pair, 0, full, full))]
            start_copy(stores, rows.at[flip, pl.ds(odd * TILE, TILE)], target)
    wait_copies(stores)


def collect_shared(full, me, blocks, so_far):
    flips = len(blocks)
    return pl.pallas_call(
        functools.partial(collect_shared_kernel, full),
        name="collect_shared",
        out_shape=bf16(*so_far.shape),
        in_specs=[IN_SMEM] + [ANYWHERE] * flips + [IN_HBM],
        out_specs=IN_HBM,
        scratch_shapes=[
            pltpu.VMEM((flips, 2 * TILE, HEAD_DIM), jnp.bfloat16),
            pltpu.SemaphoreType.DMA((flips,)),
            pltpu.SemaphoreType.DMA((2 * flips,)),
        ],
        input_output_aliases={1 + flips: 0},
        compiler_params=LEAVE_ROOM,
    )(me, *blocks, so_far)


def collect_whole_kernel(full, here, out, sems):
    stores = copy_list(sems)
    for device in range(here.shape[0]):
        for slot in range(full):
            head = head_of(device // 2, device % 2, slot, full)
            target = out.at[:, pl.ds(head * HEAD_DIM, HEAD_DIM)]
            start_copy(stores, here.at[device, pl.ds(slot * TILE, TILE)], target)
    wait_copies(stores)


def collect_whole(full, shape, here):
    return pl.pallas_call(
        functools.partial(collect_whole_kernel, full),
        name="collect_whole",
        out_shape=bf16(*shape),
        in_specs=[IN_VMEM],
        out_specs=IN_HBM,
        scratch_shapes=[pltpu.SemaphoreType.DMA((full * here.shape[0],))],
        compiler_params=LEAVE_ROOM,
    )(here)


def with_all(blocks):
    return lax.all_to_all(blocks, "seq", split_axis=0, concat_axis=0, tiled=True)


def with_partner(block, k):
    devices = lax.axis_size("seq")
    return lax.ppermute(block, "seq", [(i, i ^ (2 * k)) for i in range(devices)]) if k else block


def with_sibling(block):
    return lax.ppermute(block, "seq", [(i, i ^ 1) for i in range(lax.axis_size("seq"))])


def after(value, *others):
    return lax.optimization_barrier((value, *others))[0]


def all_after(values, *others):
    return list(lax.optimization_barrier((*values, *others))[: len(values)])


def tile_masks(full, my_index, key_tiles, key_count):
    slots = jnp.arange(full + 1)
    within = jnp.where(slots < full, slots + my_index % 2 * (full + 1), full)
    heads = my_index // 2 * (2 * full + 1) + within
    tiles, counts = key_tiles[heads], key_count[heads]
    flip = jnp.where(slots < full, 0, my_index)
    bits = jnp.left_shift(1, jnp.bitwise_xor(tiles, flip[:, None, None]))
    allowed = jnp.arange(tiles.shape[-1]) < counts[:, :, None]
    masks = jnp.sum(jnp.where(allowed, bits, 0), axis=-1)
    order = jnp.bitwise_xor(jnp.arange(tiles.shape[1])[None, :], flip[:, None])
    return jnp.take_along_axis(masks, order, axis=1)


def local_paired(queries, keys, values, q_gain, k_gain, key_tiles, key_count):
    devices = lax.axis_size("seq")
    pairs = devices // 2
    full = HEADS // devices
    my_index = lax.axis_index("seq")
    me = my_index.reshape(1)
    rest = (keys, values, q_gain, k_gain)

    whole = prepare_whole(full, devices, queries, *rest)
    masks = tile_masks(full, my_index, key_tiles, key_count)
    even, odd = prepare_shared(full, pairs, me, after(queries, masks, whole), *rest)
    whole = with_all(whole)
    shared = join_columns(even, with_partner(odd, 1))
    near, far = shared[: pairs // 4], shared[pairs // 4 :]
    near = [with_partner(block, 2 * flip) for flip, block in enumerate(near)]
    whole = after(whole, *near, *far)
    far = all_after(far, whole)
    far = [with_partner(block, 2 * flip + pairs // 2) for flip, block in enumerate(far)]
    whole_out = attend_whole(full, masks, whole)
    shared = all_after(near + far, whole_out)
    whole_back = with_all(after(whole_out, *shared))
    other = with_sibling(join_keys_values(shared))
    even, odd = attend_shared(full, masks, shared, other)
    shared_back = join_columns(even, with_partner(odd, 1))
    shared_back = [with_partner(block, 2 * flip) for flip, block in enumerate(shared_back)]
    so_far = collect_whole(full, queries.shape, whole_back)
    return collect_shared(full, me, shared_back, so_far)


def paired_fits(mesh, key_tiles_shape):
    devices = mesh.shape["seq"]
    per_pair, rest = divmod(2 * HEADS, devices)
    return (
        rest == 0
        and per_pair % 2 == 1
        and per_pair >= 3
        and devices >= 16
        and devices & (devices - 1) == 0
        and key_tiles_shape[1] == devices
        and devices <= 31
    )


def solution(mesh):
    in_specs = (
        P(("groups", "seq"), None),
        P(("groups", "seq"), None),
        P(("groups", "seq"), None),
        P(),
        P(),
        P(),
        P(),
    )
    out_specs = P(("groups", "seq"), None)

    def run(*operands):
        paired = paired_fits(mesh, operands[5].shape)
        body = local_paired if paired else local_general
        return jax.shard_map(
            body, mesh=mesh, in_specs=in_specs, out_specs=out_specs, check_vma=False
        )(*operands)

    return run
```

```python
import functools
import math

import jax
import jax.numpy as jnp
from jax import lax
from jax.experimental import pallas as pl
from jax.experimental.pallas import tpu as pltpu
from jax.sharding import PartitionSpec as P

HEADS = 40
HEAD_DIM = 128
TILE = 128


group_size = 4


def normed(rows, gain):
    values32 = rows.astype(jnp.float32)
    factor = lax.rsqrt(jnp.mean(values32 * values32, axis=-1, keepdims=True) + 1e-06)
    return (values32 * factor * gain).astype(jnp.bfloat16)


def padded(entries, length):
    return jnp.pad(entries, (0, length - entries.shape[0]), mode="edge")


def attend_units(received, slot_index, tile_index, head_index, key_tiles, key_count):

    def one_group(unit_items):
        slot_part, tile_part, head_part = unit_items
        query_rows = received[tile_part, slot_part, 0]
        key_lists = key_tiles[head_part, tile_part]
        counts = key_count[head_part, tile_part]
        key_block = received[key_lists, slot_part[:, None], 1]
        value_block = received[key_lists, slot_part[:, None], 2]
        units = query_rows.shape[0]
        tile_rows = query_rows.shape[1]
        key_flat = key_block.reshape(units, -1, key_block.shape[-1])
        value_flat = value_block.reshape(units, -1, value_block.shape[-1])
        scores = jnp.einsum(
            "uqd,ukd->uqk", query_rows, key_flat, preferred_element_type=jnp.float32
        ) / math.sqrt(query_rows.shape[-1])
        list_place = jnp.arange(key_flat.shape[1]) // tile_rows
        valid = (list_place[None, :] < counts[:, None])[:, None, :]
        masked = jnp.where(valid, scores, -jnp.inf)
        peak = jnp.max(masked, axis=-1, keepdims=True)
        weights = jnp.where(valid, jnp.exp(masked - peak), jnp.float32(0.0))
        total = jnp.sum(weights, axis=-1, keepdims=True)
        probs = weights.astype(jnp.bfloat16)
        mixed = (
            jnp.einsum("uqk,ukd->uqd", probs, value_flat, preferred_element_type=jnp.float32)
            / total
        )
        return mixed.astype(jnp.bfloat16)

    grouped = (
        slot_index.reshape(-1, group_size),
        tile_index.reshape(-1, group_size),
        head_index.reshape(-1, group_size),
    )
    result = lax.map(one_group, grouped)
    return result.reshape(-1, result.shape[2], result.shape[3])


def local_general(queries, keys, values, q_gain, k_gain, key_tiles, key_count):
    devices = lax.axis_size("seq")
    my_index = lax.axis_index("seq")
    q_normed = normed(queries, q_gain)
    k_normed = normed(keys, k_gain)
    stacked = (
        jnp.stack([q_normed, k_normed, values])
        .reshape(3, TILE, HEADS, HEAD_DIM)
        .transpose(2, 0, 1, 3)
    )
    targets = jnp.arange(devices)
    per_device = (HEADS + devices - 1) // devices
    total_slots = devices * per_device
    fewest_slots = total_slots // HEADS
    most_units = (devices + fewest_slots - 1) // fewest_slots

    def slot_layout(slot_number):
        head_of = slot_number * HEADS // total_slots
        head_start = (head_of * total_slots + HEADS - 1) // HEADS
        head_end = ((head_of + 1) * total_slots + HEADS - 1) // HEADS
        sharers = head_end - head_start
        within = slot_number - head_start
        return (head_of, within * devices // sharers, (within + 1) * devices // sharers)

    all_slots = jnp.arange(total_slots).reshape(devices, per_device)
    send_heads = slot_layout(all_slots)[0]
    received = lax.all_to_all(stacked[send_heads], "seq", split_axis=0, concat_axis=0, tiled=True)
    own_heads, lower_tile, upper_tile = slot_layout(my_index * per_device + jnp.arange(per_device))
    offsets = jnp.arange(most_units)
    tile_grid = jnp.minimum(lower_tile[:, None] + offsets[None, :], devices - 1)
    slot_grid = jnp.broadcast_to(jnp.arange(per_device)[:, None], tile_grid.shape)
    head_grid = jnp.broadcast_to(own_heads[:, None], tile_grid.shape)
    unit_total = per_device * most_units
    length = (unit_total + group_size - 1) // group_size * group_size
    finished = attend_units(
        received,
        padded(slot_grid.reshape(-1), length),
        padded(tile_grid.reshape(-1), length),
        padded(head_grid.reshape(-1), length),
        key_tiles,
        key_count,
    )[:unit_total]
    finished = finished.reshape(per_device, most_units, TILE, HEAD_DIM)
    position = targets[:, None] - lower_tile[None, :]
    inside = (position >= 0) & (targets[:, None] < upper_tile[None, :])
    gathered = finished[jnp.arange(per_device)[None, :], jnp.clip(position, 0, most_units - 1)]
    outgoing = jnp.where(inside[:, :, None, None], gathered, jnp.zeros_like(gathered))
    returned = lax.all_to_all(outgoing, "seq", split_axis=0, concat_axis=0, tiled=True)
    head_list = jnp.arange(HEADS)
    head_start = (head_list * total_slots + HEADS - 1) // HEADS
    sharers = ((head_list + 1) * total_slots + HEADS - 1) // HEADS - head_start
    owner_slot = head_start + ((my_index + 1) * sharers - 1) // devices
    pieces = returned[owner_slot // per_device, owner_slot % per_device]
    return pieces.transpose(1, 0, 2).reshape(TILE, HEADS * HEAD_DIM)


ALL_VMEM_BYTES = 60 * 1024 * 1024
IN_HBM = pl.BlockSpec(memory_space=pltpu.HBM)
ANYWHERE = pl.BlockSpec(memory_space=pl.ANY)
IN_SMEM = pl.BlockSpec(memory_space=pltpu.SMEM)
IN_VMEM = pl.BlockSpec(memory_space=pltpu.VMEM)
PARAMS = pltpu.CompilerParams(vmem_limit_bytes=ALL_VMEM_BYTES)
LEAVE_ROOM = pltpu.CompilerParams(vmem_limit_bytes=40 * 1024 * 1024)
LOADS = 2


def head_of(pair, core, slot, full):
    return pair * (2 * full + 1) + (full if slot == full else slot + core * (full + 1))


def columns_of(head):
    return slice(head * HEAD_DIM, (head + 1) * HEAD_DIM)


def traced_columns(head):
    return pl.ds(pl.multiple_of(head * HEAD_DIM, HEAD_DIM), HEAD_DIM)


def bf16(*shape):
    return jax.ShapeDtypeStruct(shape, jnp.bfloat16)


def copy_list(sems):
    return sems, []


def start_copy(copies, source, target):
    sems, started = copies
    started.append(pltpu.make_async_copy(source, target, sems.at[len(started)]))
    started[-1].start()
    return started[-1]


def wait_copies(copies):
    for copy in copies[1]:
        copy.wait()


def norm_in_place(rows, gain, loads, gain_load):
    count = TILE // len(loads)
    for part, load in enumerate(loads):
        here = slice(part * count, (part + 1) * count)
        load.wait()
        squares = jnp.zeros((count, HEAD_DIM), jnp.float32)
        for head in range(HEADS):
            block = rows[here, columns_of(head)].astype(jnp.float32)
            squares = squares + block * block
        mean = jnp.sum(squares, axis=-1, keepdims=True) / (HEADS * HEAD_DIM)
        factor = lax.rsqrt(mean + 1e-06)
        if part == 0:
            gain_load.wait()
        for head in range(HEADS):
            block = rows[here, columns_of(head)].astype(jnp.float32)
            scaled = block * factor * gain[columns_of(head)][None, :]
            rows[here, columns_of(head)] = scaled.astype(jnp.bfloat16)


def prepare_kernel(send, queries, keys, values, q_gain, k_gain, scratch):
    q_rows, k_rows, v_rows, q_scale, k_scale, in_sems = scratch
    loading = copy_list(in_sems)

    def load(source, target):
        parts = [pl.ds(i * TILE // LOADS, TILE // LOADS) for i in range(LOADS)]
        return [start_copy(loading, source.at[part], target.at[part]) for part in parts]

    k_scale_load = start_copy(loading, k_gain, k_scale)
    q_scale_load = start_copy(loading, q_gain, q_scale)
    k_loads, v_loads, q_loads = load(keys, k_rows), load(values, v_rows), load(queries, q_rows)
    norm_in_place(k_rows, k_scale, k_loads, k_scale_load)
    send(k_rows, 1)
    for part in v_loads:
        part.wait()
    send(v_rows, 2)
    norm_in_place(q_rows, q_scale, q_loads, q_scale_load)
    send(q_rows, 0)


def prepare_whole_kernel(full, *refs):
    operands, out, scratch, out_sems = refs[:5], refs[5], refs[6:-1], refs[-1]
    copies = copy_list(out_sems)

    def send(rows, tensor):
        for device in range(out.shape[0]):
            for slot in range(full):
                head = head_of(device // 2, device % 2, slot, full)
                target = out.at[device, pl.ds((3 * slot + tensor) * TILE, TILE)]
                start_copy(copies, rows.at[:, pl.ds(head * HEAD_DIM, HEAD_DIM)], target)

    prepare_kernel(send, *operands, scratch)
    wait_copies(copies)


def prepare_shared_kernel(full, me_ref, *refs):
    operands, outs, scratch, out_sems = refs[:5], refs[5:7], refs[7:-1], refs[-1]
    copies = copy_list(out_sems)

    def send(rows, tensor):
        for odd, out in enumerate(outs):
            for flip in range(out.shape[0]):
                pair = jnp.bitwise_xor(me_ref[0] // 2, 2 * flip + odd)
                target = out.at[flip, pl.ds(tensor * TILE, TILE)]
                source = rows.at[:, traced_columns(head_of(pair, 0, full, full))]
                start_copy(copies, source, target)

    prepare_kernel(send, *operands, scratch)
    wait_copies(copies)


def prepare_scratch(queries, q_gain, copies):
    rows = pltpu.VMEM(queries.shape, jnp.bfloat16)
    scale = pltpu.VMEM(q_gain.shape, jnp.float32)
    sems = pltpu.SemaphoreType.DMA
    return [rows, rows, rows, scale, scale, sems((3 * LOADS + 2,)), sems((copies,))]


def prepare_whole(full, devices, *operands):
    return pl.pallas_call(
        functools.partial(prepare_whole_kernel, full),
        name="prepare_whole",
        out_shape=bf16(devices, 3 * full * TILE, HEAD_DIM),
        in_specs=[IN_HBM] * 5,
        out_specs=ANYWHERE,
        scratch_shapes=prepare_scratch(operands[0], operands[3], 3 * full * devices),
        compiler_params=PARAMS,
    )(*operands)


def prepare_shared(full, pairs, me, *operands):
    return pl.pallas_call(
        functools.partial(prepare_shared_kernel, full),
        name="prepare_shared",
        out_shape=[bf16(pairs // 2, 3 * TILE, HEAD_DIM)] * 2,
        in_specs=[IN_SMEM] + [IN_HBM] * 5,
        out_specs=[ANYWHERE] * 2,
        scratch_shapes=prepare_scratch(operands[0], operands[3], 3 * pairs),
        compiler_params=PARAMS,
    )(me, *operands)


def join_columns_kernel(own, other, *refs):
    outs, (rows, in_sems, out_sems) = refs[:-3], refs[-3:]
    count = own.shape[1]
    loads, stores = copy_list(in_sems), copy_list(out_sems)
    for flip in range(len(outs)):
        start_copy(loads, own.at[flip], rows.at[flip, pl.ds(0, count)])
        start_copy(loads, other.at[flip], rows.at[flip, pl.ds(count, count)])
    for flip, out in enumerate(outs):
        loads[1][2 * flip].wait()
        loads[1][2 * flip + 1].wait()
        start_copy(stores, rows.at[flip], out)
    wait_copies(stores)


def join_columns(own, other):
    flips, count = own.shape[:2]
    return pl.pallas_call(
        join_columns_kernel,
        name="join_columns",
        out_shape=[bf16(2 * count, HEAD_DIM)] * flips,
        in_specs=[ANYWHERE] * 2,
        out_specs=[ANYWHERE] * flips,
        scratch_shapes=[
            pltpu.VMEM((flips, 2 * count, HEAD_DIM), jnp.bfloat16),
            pltpu.SemaphoreType.DMA((2 * flips,)),
            pltpu.SemaphoreType.DMA((flips,)),
        ],
        compiler_params=LEAVE_ROOM,
    )(own, other)


UNROLL = 4


def write_marks(marked):
    shape = (marked.shape[0], HEAD_DIM)
    tile = lax.broadcasted_iota(jnp.int32, shape, 0) // TILE
    marks = jnp.where(lax.broadcasted_iota(jnp.int32, shape, 1) == tile, 1.0, 0.0)
    marked[:, HEAD_DIM:] = marks.astype(jnp.bfloat16)


def query_masks(queries, mask):
    bit = jnp.minimum(lax.broadcasted_iota(jnp.int32, (1, HEAD_DIM), 1), 31)
    offsets = jnp.where((mask >> bit) & 1 == 1, jnp.float32(0.0), jnp.float32(-1e30))
    offsets = jnp.broadcast_to(offsets, queries.shape).astype(jnp.bfloat16)
    return jnp.concatenate([queries, offsets], axis=1)


def attend_rows(queries, keys, values, masks):
    tiles = keys.shape[0] // TILE
    marked = [query_masks(tile, mask) for tile, mask in zip(queries, masks)]
    scores = lax.dot_general(
        jnp.concatenate(marked, axis=0),
        keys,
        (((1,), (1,)), ((), ())),
        preferred_element_type=jnp.float32,
    )
    scale = jnp.float32(math.log2(math.e) / math.sqrt(HEAD_DIM))
    probs, totals = [], []
    for i in range(len(masks)):
        rows = slice(i * TILE, (i + 1) * TILE)
        parts = [scores[rows, tile * TILE : (tile + 1) * TILE] for tile in range(tiles)]
        peak = jnp.max(functools.reduce(jnp.maximum, parts), axis=-1, keepdims=True)
        weights = [jnp.exp2((part - peak) * scale) for part in parts]
        totals.append(jnp.sum(functools.reduce(jnp.add, weights), axis=-1, keepdims=True))
        probs.append(jnp.concatenate([w.astype(jnp.bfloat16) for w in weights], axis=1))
    mixed = jnp.dot(jnp.concatenate(probs, axis=0), values, preferred_element_type=jnp.float32)
    return [
        (mixed[i * TILE : (i + 1) * TILE] / total).astype(jnp.bfloat16)
        for i, total in enumerate(totals)
    ]


def attend_slot(mask_ref, slot, here, first, out, out_first, start, stride, together, marked, stored):
    def part(tile, tensor):
        return here[tile, first + tensor * TILE : first + (tensor + 1) * TILE]

    marked[:, :HEAD_DIM] = part(slice(None), 1).reshape(-1, HEAD_DIM)

    products = here.shape[0] // (stride * together)
    unroll = math.gcd(products, UNROLL)

    def step(index, carry):
        for product in range(unroll):
            at = (index * unroll + product) * together
            tiles = [start + (at + i) * stride for i in range(together)]
            values = part(slice(None), 2).reshape(-1, HEAD_DIM)
            masks = [mask_ref[slot, tile] for tile in tiles]
            blocks = attend_rows([part(tile, 0) for tile in tiles], marked[...], values, masks)
            for tile, block in zip(tiles, blocks):
                out[tile, out_first : out_first + TILE] = block
            stored(at)
        return carry

    for index in range(products // unroll):
        step(index, 0)


def marked_keys(devices):
    return pltpu.VMEM((devices * TILE, 2 * HEAD_DIM), jnp.bfloat16)


def attend_whole_kernel(full, mask_ref, here, outs, out, marked, sems):
    stores = copy_list(sems)
    write_marks(marked)
    for slot in range(full):
        rows = pl.ds(slot * TILE, TILE)

        def stored(tile, rows=rows):
            tiles = pl.ds(tile, 4)
            start_copy(stores, out.at[tiles, rows], outs.at[tiles, rows])

        attend_slot(mask_ref, slot, here, 3 * slot * TILE, out, slot * TILE, 0, 1, 4, marked, stored)
    wait_copies(stores)


def attend_whole(full, masks, here):
    shape = (here.shape[0], full * TILE, HEAD_DIM)
    return pl.pallas_call(
        functools.partial(attend_whole_kernel, full),
        name="attend_whole",
        out_shape=bf16(*shape),
        in_specs=[IN_SMEM, IN_VMEM],
        out_specs=IN_HBM,
        scratch_shapes=[
            pltpu.VMEM(shape, jnp.bfloat16),
            marked_keys(here.shape[0]),
            pltpu.SemaphoreType.DMA((full * here.shape[0] // 4,)),
        ],
        compiler_params=PARAMS,
    )(masks, here)


def attend_shared_kernel(full, odd, mask_ref, *refs):
    blocks, (other, outs), scratch = refs[:-7], refs[-7:-5], refs[-5:]
    here, out, marked, in_sems, out_sems = scratch
    loads, stores = copy_list(in_sems), copy_list(out_sems)
    for flip, block in enumerate(blocks):
        for second in range(2):
            partner = 2 * flip + second
            start_copy(loads, block.at[pl.ds(3 * second * TILE, 3 * TILE)], here.at[2 * partner])
            target = here.at[2 * partner + 1, pl.ds(TILE, 2 * TILE)]
            start_copy(loads, other.at[partner], target)
    write_marks(marked)
    wait_copies(loads)
    attend_slot(mask_ref, full, here, 0, out, 0, 2 * odd, 4, 4, marked, lambda tile: None)
    for flip in range(len(blocks)):
        start_copy(stores, out.at[2 * (2 * flip + odd)], outs.at[flip])
    wait_copies(stores)


def attend_shared(full, odd, masks, blocks, other):
    flips = len(blocks)
    return pl.pallas_call(
        functools.partial(attend_shared_kernel, full, odd),
        name="attend_shared",
        out_shape=bf16(flips, TILE, HEAD_DIM),
        in_specs=[IN_SMEM] + [ANYWHERE] * (flips + 1),
        out_specs=ANYWHERE,
        scratch_shapes=[
            pltpu.VMEM((4 * flips, 3 * TILE, HEAD_DIM), jnp.bfloat16),
            pltpu.VMEM((4 * flips, TILE, HEAD_DIM), jnp.bfloat16),
            marked_keys(4 * flips),
            pltpu.SemaphoreType.DMA((4 * flips,)),
            pltpu.SemaphoreType.DMA((flips,)),
        ],
        compiler_params=LEAVE_ROOM,
    )(masks, *blocks, other)


def join_keys_values_kernel(*refs):
    blocks, (out, rows, in_sems, out_sems) = refs[:-4], refs[-4:]
    loads, stores = copy_list(in_sems), copy_list(out_sems)
    for partner in range(2 * len(blocks)):
        source = blocks[partner // 2].at[pl.ds((3 * (partner % 2) + 1) * TILE, 2 * TILE)]
        start_copy(loads, source, rows.at[partner])
    for partner, load in enumerate(loads[1]):
        load.wait()
        start_copy(stores, rows.at[partner], out.at[partner])
    wait_copies(stores)


def join_keys_values(blocks):
    shape = (2 * len(blocks), 2 * TILE, HEAD_DIM)
    sems = pltpu.SemaphoreType.DMA((2 * len(blocks),))
    return pl.pallas_call(
        join_keys_values_kernel,
        name="join_keys_values",
        out_shape=bf16(*shape),
        in_specs=[ANYWHERE] * len(blocks),
        out_specs=ANYWHERE,
        scratch_shapes=[pltpu.VMEM(shape, jnp.bfloat16), sems, sems],
        compiler_params=LEAVE_ROOM,
    )(*blocks)


def collect_shared_kernel(full, me_ref, *refs):
    blocks, (_, out, rows, in_sems, out_sems) = refs[:-5], refs[-5:]
    loads, stores = copy_list(in_sems), copy_list(out_sems)
    for flip, block in enumerate(blocks):
        start_copy(loads, block, rows.at[flip])
    for flip, load in enumerate(loads[1]):
        load.wait()
        for odd in range(2):
            pair = jnp.bitwise_xor(me_ref[0] // 2, 2 * flip + odd)
            target = out.at[:, traced_columns(head_of(pair, 0, full, full))]
            start_copy(stores, rows.at[flip, pl.ds(odd * TILE, TILE)], target)
    wait_copies(stores)


def collect_shared(full, me, blocks, so_far):
    flips = len(blocks)
    return pl.pallas_call(
        functools.partial(collect_shared_kernel, full),
        name="collect_shared",
        out_shape=bf16(*so_far.shape),
        in_specs=[IN_SMEM] + [ANYWHERE] * flips + [IN_HBM],
        out_specs=IN_HBM,
        scratch_shapes=[
            pltpu.VMEM((flips, 2 * TILE, HEAD_DIM), jnp.bfloat16),
            pltpu.SemaphoreType.DMA((flips,)),
            pltpu.SemaphoreType.DMA((2 * flips,)),
        ],
        input_output_aliases={1 + flips: 0},
        compiler_params=LEAVE_ROOM,
    )(me, *blocks, so_far)


def collect_whole_kernel(full, here, out, sems):
    stores = copy_list(sems)
    for device in range(here.shape[0]):
        for slot in range(full):
            head = head_of(device // 2, device % 2, slot, full)
            target = out.at[:, pl.ds(head * HEAD_DIM, HEAD_DIM)]
            start_copy(stores, here.at[device, pl.ds(slot * TILE, TILE)], target)
    wait_copies(stores)


def collect_whole(full, shape, here):
    return pl.pallas_call(
        functools.partial(collect_whole_kernel, full),
        name="collect_whole",
        out_shape=bf16(*shape),
        in_specs=[IN_VMEM],
        out_specs=IN_HBM,
        scratch_shapes=[pltpu.SemaphoreType.DMA((full * here.shape[0],))],
        compiler_params=LEAVE_ROOM,
    )(here)


def with_all(blocks):
    return lax.all_to_all(blocks, "seq", split_axis=0, concat_axis=0, tiled=True)


def with_partner(block, k):
    devices = lax.axis_size("seq")
    return lax.ppermute(block, "seq", [(i, i ^ (2 * k)) for i in range(devices)]) if k else block


def with_sibling(block):
    return lax.ppermute(block, "seq", [(i, i ^ 1) for i in range(lax.axis_size("seq"))])


def after(value, *others):
    return lax.optimization_barrier((value, *others))[0]


def all_after(values, *others):
    return list(lax.optimization_barrier((*values, *others))[: len(values)])


def tile_masks(full, my_index, key_tiles, key_count):
    slots = jnp.arange(full + 1)
    within = jnp.where(slots < full, slots + my_index % 2 * (full + 1), full)
    heads = my_index // 2 * (2 * full + 1) + within
    tiles, counts = key_tiles[heads], key_count[heads]
    flip = jnp.where(slots < full, 0, my_index)
    bits = jnp.left_shift(1, jnp.bitwise_xor(tiles, flip[:, None, None]))
    allowed = jnp.arange(tiles.shape[-1]) < counts[:, :, None]
    masks = jnp.sum(jnp.where(allowed, bits, 0), axis=-1)
    order = jnp.bitwise_xor(jnp.arange(tiles.shape[1])[None, :], flip[:, None])
    return jnp.take_along_axis(masks, order, axis=1)


def local_paired(queries, keys, values, q_gain, k_gain, key_tiles, key_count):
    devices = lax.axis_size("seq")
    pairs = devices // 2
    full = HEADS // devices
    my_index = lax.axis_index("seq")
    me = my_index.reshape(1)
    rest = (keys, values, q_gain, k_gain)

    whole = prepare_whole(full, devices, queries, *rest)
    masks = tile_masks(full, my_index, key_tiles, key_count)
    even, odd = prepare_shared(full, pairs, me, after(queries, masks, whole), *rest)
    whole = with_all(whole)
    shared = join_columns(even, with_partner(odd, 1))
    near, far = shared[: pairs // 4], shared[pairs // 4 :]
    near = [with_partner(block, 2 * flip) for flip, block in enumerate(near)]
    whole = after(whole, *near, *far)
    far = all_after(far, whole)
    far = [with_partner(block, 2 * flip + pairs // 2) for flip, block in enumerate(far)]
    whole_out = attend_whole(full, masks, whole)
    shared = all_after(near + far, whole_out)
    whole_back = with_all(after(whole_out, *shared))
    other = with_sibling(join_keys_values(shared))
    odd = attend_shared(full, 1, masks, shared, other)
    even = attend_shared(full, 0, masks, shared, after(other, odd))
    shared_back = join_columns(even, with_partner(odd, 1))
    shared_back = [with_partner(block, 2 * flip) for flip, block in enumerate(shared_back)]
    so_far = collect_whole(full, queries.shape, whole_back)
    return collect_shared(full, me, shared_back, so_far)


def paired_fits(mesh, key_tiles_shape):
    devices = mesh.shape["seq"]
    per_pair, rest = divmod(2 * HEADS, devices)
    return (
        rest == 0
        and per_pair % 2 == 1
        and per_pair >= 3
        and devices >= 16
        and devices & (devices - 1) == 0
        and key_tiles_shape[1] == devices
        and devices <= 31
    )


def solution(mesh):
    in_specs = (
        P(("groups", "seq"), None),
        P(("groups", "seq"), None),
        P(("groups", "seq"), None),
        P(),
        P(),
        P(),
        P(),
    )
    out_specs = P(("groups", "seq"), None)

    def run(*operands):
        paired = paired_fits(mesh, operands[5].shape)
        body = local_paired if paired else local_general
        return jax.shard_map(
            body, mesh=mesh, in_specs=in_specs, out_specs=out_specs, check_vma=False
        )(*operands)

    return run
```

```python
import functools
import math

import jax
import jax.numpy as jnp
from jax import lax
from jax.experimental import pallas as pl
from jax.experimental.pallas import tpu as pltpu
from jax.sharding import PartitionSpec as P

HEADS = 40
HEAD_DIM = 128
TILE = 128


group_size = 4


def normed(rows, gain):
    values32 = rows.astype(jnp.float32)
    factor = lax.rsqrt(jnp.mean(values32 * values32, axis=-1, keepdims=True) + 1e-06)
    return (values32 * factor * gain).astype(jnp.bfloat16)


def padded(entries, length):
    return jnp.pad(entries, (0, length - entries.shape[0]), mode="edge")


def attend_units(received, slot_index, tile_index, head_index, key_tiles, key_count):

    def one_group(unit_items):
        slot_part, tile_part, head_part = unit_items
        query_rows = received[tile_part, slot_part, 0]
        key_lists = key_tiles[head_part, tile_part]
        counts = key_count[head_part, tile_part]
        key_block = received[key_lists, slot_part[:, None], 1]
        value_block = received[key_lists, slot_part[:, None], 2]
        units = query_rows.shape[0]
        tile_rows = query_rows.shape[1]
        key_flat = key_block.reshape(units, -1, key_block.shape[-1])
        value_flat = value_block.reshape(units, -1, value_block.shape[-1])
        scores = jnp.einsum(
            "uqd,ukd->uqk", query_rows, key_flat, preferred_element_type=jnp.float32
        ) / math.sqrt(query_rows.shape[-1])
        list_place = jnp.arange(key_flat.shape[1]) // tile_rows
        valid = (list_place[None, :] < counts[:, None])[:, None, :]
        masked = jnp.where(valid, scores, -jnp.inf)
        peak = jnp.max(masked, axis=-1, keepdims=True)
        weights = jnp.where(valid, jnp.exp(masked - peak), jnp.float32(0.0))
        total = jnp.sum(weights, axis=-1, keepdims=True)
        probs = weights.astype(jnp.bfloat16)
        mixed = (
            jnp.einsum("uqk,ukd->uqd", probs, value_flat, preferred_element_type=jnp.float32)
            / total
        )
        return mixed.astype(jnp.bfloat16)

    grouped = (
        slot_index.reshape(-1, group_size),
        tile_index.reshape(-1, group_size),
        head_index.reshape(-1, group_size),
    )
    result = lax.map(one_group, grouped)
    return result.reshape(-1, result.shape[2], result.shape[3])


def local_general(queries, keys, values, q_gain, k_gain, key_tiles, key_count):
    devices = lax.axis_size("seq")
    my_index = lax.axis_index("seq")
    q_normed = normed(queries, q_gain)
    k_normed = normed(keys, k_gain)
    stacked = (
        jnp.stack([q_normed, k_normed, values])
        .reshape(3, TILE, HEADS, HEAD_DIM)
        .transpose(2, 0, 1, 3)
    )
    targets = jnp.arange(devices)
    per_device = (HEADS + devices - 1) // devices
    total_slots = devices * per_device
    fewest_slots = total_slots // HEADS
    most_units = (devices + fewest_slots - 1) // fewest_slots

    def slot_layout(slot_number):
        head_of = slot_number * HEADS // total_slots
        head_start = (head_of * total_slots + HEADS - 1) // HEADS
        head_end = ((head_of + 1) * total_slots + HEADS - 1) // HEADS
        sharers = head_end - head_start
        within = slot_number - head_start
        return (head_of, within * devices // sharers, (within + 1) * devices // sharers)

    all_slots = jnp.arange(total_slots).reshape(devices, per_device)
    send_heads = slot_layout(all_slots)[0]
    received = lax.all_to_all(stacked[send_heads], "seq", split_axis=0, concat_axis=0, tiled=True)
    own_heads, lower_tile, upper_tile = slot_layout(my_index * per_device + jnp.arange(per_device))
    offsets = jnp.arange(most_units)
    tile_grid = jnp.minimum(lower_tile[:, None] + offsets[None, :], devices - 1)
    slot_grid = jnp.broadcast_to(jnp.arange(per_device)[:, None], tile_grid.shape)
    head_grid = jnp.broadcast_to(own_heads[:, None], tile_grid.shape)
    unit_total = per_device * most_units
    length = (unit_total + group_size - 1) // group_size * group_size
    finished = attend_units(
        received,
        padded(slot_grid.reshape(-1), length),
        padded(tile_grid.reshape(-1), length),
        padded(head_grid.reshape(-1), length),
        key_tiles,
        key_count,
    )[:unit_total]
    finished = finished.reshape(per_device, most_units, TILE, HEAD_DIM)
    position = targets[:, None] - lower_tile[None, :]
    inside = (position >= 0) & (targets[:, None] < upper_tile[None, :])
    gathered = finished[jnp.arange(per_device)[None, :], jnp.clip(position, 0, most_units - 1)]
    outgoing = jnp.where(inside[:, :, None, None], gathered, jnp.zeros_like(gathered))
    returned = lax.all_to_all(outgoing, "seq", split_axis=0, concat_axis=0, tiled=True)
    head_list = jnp.arange(HEADS)
    head_start = (head_list * total_slots + HEADS - 1) // HEADS
    sharers = ((head_list + 1) * total_slots + HEADS - 1) // HEADS - head_start
    owner_slot = head_start + ((my_index + 1) * sharers - 1) // devices
    pieces = returned[owner_slot // per_device, owner_slot % per_device]
    return pieces.transpose(1, 0, 2).reshape(TILE, HEADS * HEAD_DIM)


ALL_VMEM_BYTES = 60 * 1024 * 1024
IN_HBM = pl.BlockSpec(memory_space=pltpu.HBM)
ANYWHERE = pl.BlockSpec(memory_space=pl.ANY)
IN_SMEM = pl.BlockSpec(memory_space=pltpu.SMEM)
IN_VMEM = pl.BlockSpec(memory_space=pltpu.VMEM)
PARAMS = pltpu.CompilerParams(vmem_limit_bytes=ALL_VMEM_BYTES)
LEAVE_ROOM = pltpu.CompilerParams(vmem_limit_bytes=40 * 1024 * 1024)
LOADS = 2


def head_of(pair, core, slot, full):
    return pair * (2 * full + 1) + (full if slot == full else slot + core * (full + 1))


def columns_of(head):
    return slice(head * HEAD_DIM, (head + 1) * HEAD_DIM)


def traced_columns(head):
    return pl.ds(pl.multiple_of(head * HEAD_DIM, HEAD_DIM), HEAD_DIM)


def bf16(*shape):
    return jax.ShapeDtypeStruct(shape, jnp.bfloat16)


def copy_list(sems):
    return sems, []


def start_copy(copies, source, target):
    sems, started = copies
    started.append(pltpu.make_async_copy(source, target, sems.at[len(started)]))
    started[-1].start()
    return started[-1]


def wait_copies(copies):
    for copy in copies[1]:
        copy.wait()


def norm_in_place(rows, gain, loads, gain_load):
    count = TILE // len(loads)
    for part, load in enumerate(loads):
        here = slice(part * count, (part + 1) * count)
        load.wait()
        squares = jnp.zeros((count, HEAD_DIM), jnp.float32)
        for head in range(HEADS):
            block = rows[here, columns_of(head)].astype(jnp.float32)
            squares = squares + block * block
        mean = jnp.sum(squares, axis=-1, keepdims=True) / (HEADS * HEAD_DIM)
        factor = lax.rsqrt(mean + 1e-06)
        if part == 0:
            gain_load.wait()
        for head in range(HEADS):
            block = rows[here, columns_of(head)].astype(jnp.float32)
            scaled = block * factor * gain[columns_of(head)][None, :]
            rows[here, columns_of(head)] = scaled.astype(jnp.bfloat16)


def prepare_kernel(send, queries, keys, values, q_gain, k_gain, scratch):
    q_rows, k_rows, v_rows, q_scale, k_scale, in_sems = scratch
    loading = copy_list(in_sems)

    def load(source, target):
        parts = [pl.ds(i * TILE // LOADS, TILE // LOADS) for i in range(LOADS)]
        return [start_copy(loading, source.at[part], target.at[part]) for part in parts]

    k_scale_load = start_copy(loading, k_gain, k_scale)
    q_scale_load = start_copy(loading, q_gain, q_scale)
    k_loads, v_loads, q_loads = load(keys, k_rows), load(values, v_rows), load(queries, q_rows)
    norm_in_place(k_rows, k_scale, k_loads, k_scale_load)
    send(k_rows, 1)
    for part in v_loads:
        part.wait()
    send(v_rows, 2)
    norm_in_place(q_rows, q_scale, q_loads, q_scale_load)
    send(q_rows, 0)


def prepare_whole_kernel(full, *refs):
    operands, out, scratch, out_sems = refs[:5], refs[5], refs[6:-1], refs[-1]
    copies = copy_list(out_sems)

    def send(rows, tensor):
        for device in range(out.shape[0]):
            for slot in range(full):
                head = head_of(device // 2, device % 2, slot, full)
                target = out.at[device, pl.ds((3 * slot + tensor) * TILE, TILE)]
                start_copy(copies, rows.at[:, pl.ds(head * HEAD_DIM, HEAD_DIM)], target)

    prepare_kernel(send, *operands, scratch)
    wait_copies(copies)


def prepare_shared_kernel(full, me_ref, *refs):
    operands, outs, scratch, out_sems = refs[:5], refs[5:7], refs[7:-1], refs[-1]
    copies = copy_list(out_sems)

    def send(rows, tensor):
        for odd, out in enumerate(outs):
            for flip in range(out.shape[0]):
                pair = jnp.bitwise_xor(me_ref[0] // 2, 2 * flip + odd)
                target = out.at[flip, pl.ds(tensor * TILE, TILE)]
                source = rows.at[:, traced_columns(head_of(pair, 0, full, full))]
                start_copy(copies, source, target)

    prepare_kernel(send, *operands, scratch)
    wait_copies(copies)


def prepare_scratch(queries, q_gain, copies):
    rows = pltpu.VMEM(queries.shape, jnp.bfloat16)
    scale = pltpu.VMEM(q_gain.shape, jnp.float32)
    sems = pltpu.SemaphoreType.DMA
    return [rows, rows, rows, scale, scale, sems((3 * LOADS + 2,)), sems((copies,))]


def prepare_whole(full, devices, *operands):
    return pl.pallas_call(
        functools.partial(prepare_whole_kernel, full),
        name="prepare_whole",
        out_shape=bf16(devices, 3 * full * TILE, HEAD_DIM),
        in_specs=[IN_HBM] * 5,
        out_specs=ANYWHERE,
        scratch_shapes=prepare_scratch(operands[0], operands[3], 3 * full * devices),
        compiler_params=PARAMS,
    )(*operands)


def prepare_shared(full, pairs, me, *operands):
    return pl.pallas_call(
        functools.partial(prepare_shared_kernel, full),
        name="prepare_shared",
        out_shape=[bf16(pairs // 2, 3 * TILE, HEAD_DIM)] * 2,
        in_specs=[IN_SMEM] + [IN_HBM] * 5,
        out_specs=[ANYWHERE] * 2,
        scratch_shapes=prepare_scratch(operands[0], operands[3], 3 * pairs),
        compiler_params=PARAMS,
    )(me, *operands)


def join_columns_kernel(own, other, *refs):
    outs, (rows, in_sems, out_sems) = refs[:-3], refs[-3:]
    count = own.shape[1]
    loads, stores = copy_list(in_sems), copy_list(out_sems)
    for flip in range(len(outs)):
        start_copy(loads, own.at[flip], rows.at[flip, pl.ds(0, count)])
        start_copy(loads, other.at[flip], rows.at[flip, pl.ds(count, count)])
    for flip, out in enumerate(outs):
        loads[1][2 * flip].wait()
        loads[1][2 * flip + 1].wait()
        start_copy(stores, rows.at[flip], out)
    wait_copies(stores)


def join_columns(own, other):
    flips, count = own.shape[:2]
    return pl.pallas_call(
        join_columns_kernel,
        name="join_columns",
        out_shape=[bf16(2 * count, HEAD_DIM)] * flips,
        in_specs=[ANYWHERE] * 2,
        out_specs=[ANYWHERE] * flips,
        scratch_shapes=[
            pltpu.VMEM((flips, 2 * count, HEAD_DIM), jnp.bfloat16),
            pltpu.SemaphoreType.DMA((2 * flips,)),
            pltpu.SemaphoreType.DMA((flips,)),
        ],
        compiler_params=LEAVE_ROOM,
    )(own, other)


UNROLL = 4


def write_marks(marked):
    shape = (marked.shape[0], HEAD_DIM)
    tile = lax.broadcasted_iota(jnp.int32, shape, 0) // TILE
    marks = jnp.where(lax.broadcasted_iota(jnp.int32, shape, 1) == tile, 1.0, 0.0)
    marked[:, HEAD_DIM:] = marks.astype(jnp.bfloat16)


def query_masks(queries, mask):
    bit = jnp.minimum(lax.broadcasted_iota(jnp.int32, (1, HEAD_DIM), 1), 31)
    offsets = jnp.where((mask >> bit) & 1 == 1, jnp.float32(0.0), jnp.float32(-1e30))
    offsets = jnp.broadcast_to(offsets, queries.shape).astype(jnp.bfloat16)
    return jnp.concatenate([queries, offsets], axis=1)


def attend_rows(queries, keys, values, masks):
    tiles = keys.shape[0] // TILE
    marked = [query_masks(tile, mask) for tile, mask in zip(queries, masks)]
    scores = lax.dot_general(
        jnp.concatenate(marked, axis=0),
        keys,
        (((1,), (1,)), ((), ())),
        preferred_element_type=jnp.float32,
    )
    scale = jnp.float32(math.log2(math.e) / math.sqrt(HEAD_DIM))
    probs, totals = [], []
    for i in range(len(masks)):
        rows = slice(i * TILE, (i + 1) * TILE)
        parts = [scores[rows, tile * TILE : (tile + 1) * TILE] for tile in range(tiles)]
        peak = jnp.max(functools.reduce(jnp.maximum, parts), axis=-1, keepdims=True)
        weights = [jnp.exp2((part - peak) * scale) for part in parts]
        totals.append(jnp.sum(functools.reduce(jnp.add, weights), axis=-1, keepdims=True))
        probs.append(jnp.concatenate([w.astype(jnp.bfloat16) for w in weights], axis=1))
    mixed = jnp.dot(jnp.concatenate(probs, axis=0), values, preferred_element_type=jnp.float32)
    return [
        (mixed[i * TILE : (i + 1) * TILE] / total).astype(jnp.bfloat16)
        for i, total in enumerate(totals)
    ]


def attend_slot(mask_ref, slot, here, first, out, out_first, stride, together, marked, stored):
    def part(tile, tensor):
        return here[tile, first + tensor * TILE : first + (tensor + 1) * TILE]

    marked[:, :HEAD_DIM] = part(slice(None), 1).reshape(-1, HEAD_DIM)

    products = here.shape[0] // (stride * together)
    unroll = math.gcd(products, UNROLL)

    def step(index, carry):
        for product in range(unroll):
            at = (index * unroll + product) * together
            tiles = [(at + i) * stride for i in range(together)]
            values = part(slice(None), 2).reshape(-1, HEAD_DIM)
            masks = [mask_ref[slot, tile] for tile in tiles]
            blocks = attend_rows([part(tile, 0) for tile in tiles], marked[...], values, masks)
            for tile, block in zip(tiles, blocks):
                out[tile, out_first : out_first + TILE] = block
            stored(at)
        return carry

    for index in range(products // unroll):
        step(index, 0)


def marked_keys(devices):
    return pltpu.VMEM((devices * TILE, 2 * HEAD_DIM), jnp.bfloat16)


def attend_whole_kernel(full, mask_ref, here, outs, out, marked, sems):
    stores = copy_list(sems)
    write_marks(marked)
    for slot in range(full):
        rows = pl.ds(slot * TILE, TILE)

        def stored(tile, rows=rows):
            tiles = pl.ds(tile, 4)
            start_copy(stores, out.at[tiles, rows], outs.at[tiles, rows])

        attend_slot(mask_ref, slot, here, 3 * slot * TILE, out, slot * TILE, 1, 4, marked, stored)
    wait_copies(stores)


def attend_whole(full, masks, here):
    shape = (here.shape[0], full * TILE, HEAD_DIM)
    return pl.pallas_call(
        functools.partial(attend_whole_kernel, full),
        name="attend_whole",
        out_shape=bf16(*shape),
        in_specs=[IN_SMEM, IN_VMEM],
        out_specs=IN_HBM,
        scratch_shapes=[
            pltpu.VMEM(shape, jnp.bfloat16),
            marked_keys(here.shape[0]),
            pltpu.SemaphoreType.DMA((full * here.shape[0] // 4,)),
        ],
        compiler_params=PARAMS,
    )(masks, here)


def attend_shared_kernel(full, mask_ref, *refs):
    blocks, (other, *outs), scratch = refs[:-8], refs[-8:-5], refs[-5:]
    here, out, marked, in_sems, out_sems = scratch
    loads, stores = copy_list(in_sems), copy_list(out_sems)
    for flip, block in enumerate(blocks):
        for odd in range(2):
            partner = 2 * flip + odd
            start_copy(loads, block.at[pl.ds(3 * odd * TILE, 3 * TILE)], here.at[2 * partner])
            target = here.at[2 * partner + 1, pl.ds(TILE, 2 * TILE)]
            start_copy(loads, other.at[partner], target)
    write_marks(marked)
    wait_copies(loads)
    attend_slot(mask_ref, full, here, 0, out, 0, 2, 2, marked, lambda tile: None)
    for flip in range(len(blocks)):
        for odd in range(2):
            start_copy(stores, out.at[2 * (2 * flip + odd)], outs[odd].at[flip])
    wait_copies(stores)


def attend_shared(full, masks, blocks, other):
    flips = len(blocks)
    return pl.pallas_call(
        functools.partial(attend_shared_kernel, full),
        name="attend_shared",
        out_shape=[bf16(flips, TILE, HEAD_DIM)] * 2,
        in_specs=[IN_SMEM] + [ANYWHERE] * (flips + 1),
        out_specs=[ANYWHERE] * 2,
        scratch_shapes=[
            pltpu.VMEM((4 * flips, 3 * TILE, HEAD_DIM), jnp.bfloat16),
            pltpu.VMEM((4 * flips, TILE, HEAD_DIM), jnp.bfloat16),
            marked_keys(4 * flips),
            pltpu.SemaphoreType.DMA((4 * flips,)),
            pltpu.SemaphoreType.DMA((2 * flips,)),
        ],
        compiler_params=LEAVE_ROOM,
    )(masks, *blocks, other)


def join_keys_values_kernel(*refs):
    blocks, (out, rows, in_sems, out_sems) = refs[:-4], refs[-4:]
    loads, stores = copy_list(in_sems), copy_list(out_sems)
    for partner in range(2 * len(blocks)):
        source = blocks[partner // 2].at[pl.ds((3 * (partner % 2) + 1) * TILE, 2 * TILE)]
        start_copy(loads, source, rows.at[partner])
    for partner, load in enumerate(loads[1]):
        load.wait()
        start_copy(stores, rows.at[partner], out.at[partner])
    wait_copies(stores)


def join_keys_values(blocks):
    shape = (2 * len(blocks), 2 * TILE, HEAD_DIM)
    sems = pltpu.SemaphoreType.DMA((2 * len(blocks),))
    return pl.pallas_call(
        join_keys_values_kernel,
        name="join_keys_values",
        out_shape=bf16(*shape),
        in_specs=[ANYWHERE] * len(blocks),
        out_specs=ANYWHERE,
        scratch_shapes=[pltpu.VMEM(shape, jnp.bfloat16), sems, sems],
        compiler_params=LEAVE_ROOM,
    )(*blocks)


def collect_shared_kernel(full, me_ref, *refs):
    blocks, (_, out, rows, in_sems, out_sems) = refs[:-5], refs[-5:]
    loads, stores = copy_list(in_sems), copy_list(out_sems)
    for flip, block in enumerate(blocks):
        start_copy(loads, block, rows.at[flip])
    for flip, load in enumerate(loads[1]):
        load.wait()
        for odd in range(2):
            pair = jnp.bitwise_xor(me_ref[0] // 2, 2 * flip + odd)
            target = out.at[:, traced_columns(head_of(pair, 0, full, full))]
            start_copy(stores, rows.at[flip, pl.ds(odd * TILE, TILE)], target)
    wait_copies(stores)


def collect_shared(full, me, blocks, so_far):
    flips = len(blocks)
    return pl.pallas_call(
        functools.partial(collect_shared_kernel, full),
        name="collect_shared",
        out_shape=bf16(*so_far.shape),
        in_specs=[IN_SMEM] + [ANYWHERE] * flips + [IN_HBM],
        out_specs=IN_HBM,
        scratch_shapes=[
            pltpu.VMEM((flips, 2 * TILE, HEAD_DIM), jnp.bfloat16),
            pltpu.SemaphoreType.DMA((flips,)),
            pltpu.SemaphoreType.DMA((2 * flips,)),
        ],
        input_output_aliases={1 + flips: 0},
        compiler_params=LEAVE_ROOM,
    )(me, *blocks, so_far)


def collect_whole_kernel(full, here, out, sems):
    stores = copy_list(sems)
    for device in range(here.shape[0]):
        for slot in range(full):
            head = head_of(device // 2, device % 2, slot, full)
            target = out.at[:, pl.ds(head * HEAD_DIM, HEAD_DIM)]
            start_copy(stores, here.at[device, pl.ds(slot * TILE, TILE)], target)
    wait_copies(stores)


def collect_whole(full, shape, here):
    return pl.pallas_call(
        functools.partial(collect_whole_kernel, full),
        name="collect_whole",
        out_shape=bf16(*shape),
        in_specs=[IN_VMEM],
        out_specs=IN_HBM,
        scratch_shapes=[pltpu.SemaphoreType.DMA((full * here.shape[0],))],
        compiler_params=LEAVE_ROOM,
    )(here)


def with_all(blocks):
    return lax.all_to_all(blocks, "seq", split_axis=0, concat_axis=0, tiled=True)


def with_partner(block, k):
    devices = lax.axis_size("seq")
    return lax.ppermute(block, "seq", [(i, i ^ (2 * k)) for i in range(devices)]) if k else block


def with_sibling(block):
    return lax.ppermute(block, "seq", [(i, i ^ 1) for i in range(lax.axis_size("seq"))])


def after(value, *others):
    return lax.optimization_barrier((value, *others))[0]


def all_after(values, *others):
    return list(lax.optimization_barrier((*values, *others))[: len(values)])


def tile_masks(full, my_index, key_tiles, key_count):
    slots = jnp.arange(full + 1)
    within = jnp.where(slots < full, slots + my_index % 2 * (full + 1), full)
    heads = my_index // 2 * (2 * full + 1) + within
    tiles, counts = key_tiles[heads], key_count[heads]
    flip = jnp.where(slots < full, 0, my_index)
    bits = jnp.left_shift(1, jnp.bitwise_xor(tiles, flip[:, None, None]))
    allowed = jnp.arange(tiles.shape[-1]) < counts[:, :, None]
    masks = jnp.sum(jnp.where(allowed, bits, 0), axis=-1)
    order = jnp.bitwise_xor(jnp.arange(tiles.shape[1])[None, :], flip[:, None])
    return jnp.take_along_axis(masks, order, axis=1)


def local_paired(queries, keys, values, q_gain, k_gain, key_tiles, key_count):
    devices = lax.axis_size("seq")
    pairs = devices // 2
    full = HEADS // devices
    my_index = lax.axis_index("seq")
    me = my_index.reshape(1)
    rest = (keys, values, q_gain, k_gain)

    whole = prepare_whole(full, devices, queries, *rest)
    masks = tile_masks(full, my_index, key_tiles, key_count)
    even, odd = prepare_shared(full, pairs, me, after(queries, masks, whole), *rest)
    whole = with_all(whole)
    shared = join_columns(even, with_partner(odd, 1))
    near, far = shared[: pairs // 4], shared[pairs // 4 :]
    near = [with_partner(block, 2 * flip) for flip, block in enumerate(near)]
    whole = after(whole, *far)
    far = all_after(far, whole)
    far = [with_partner(block, 2 * flip + pairs // 2) for flip, block in enumerate(far)]
    whole_out = attend_whole(full, masks, whole)
    shared = all_after(near + far, whole_out)
    whole_back = with_all(after(whole_out, *shared))
    other = with_sibling(join_keys_values(shared))
    even, odd = attend_shared(full, masks, shared, other)
    shared_back = join_columns(even, with_partner(odd, 1))
    shared_back = [with_partner(block, 2 * flip) for flip, block in enumerate(shared_back)]
    so_far = collect_whole(full, queries.shape, whole_back)
    return collect_shared(full, me, shared_back, so_far)


def paired_fits(mesh, key_tiles_shape):
    devices = mesh.shape["seq"]
    per_pair, rest = divmod(2 * HEADS, devices)
    return (
        rest == 0
        and per_pair % 2 == 1
        and per_pair >= 3
        and devices >= 16
        and devices & (devices - 1) == 0
        and key_tiles_shape[1] == devices
        and devices <= 31
    )


def solution(mesh):
    in_specs = (
        P(("groups", "seq"), None),
        P(("groups", "seq"), None),
        P(("groups", "seq"), None),
        P(),
        P(),
        P(),
        P(),
    )
    out_specs = P(("groups", "seq"), None)

    def run(*operands):
        paired = paired_fits(mesh, operands[5].shape)
        body = local_paired if paired else local_general
        return jax.shard_map(
            body, mesh=mesh, in_specs=in_specs, out_specs=out_specs, check_vma=False
        )(*operands)

    return run
```
